128 devices in a mesh: band: 16 (over z, x_hi, core), dom: 8 (over y, x_lo).
Axes of the slice: x: 4 (x_hi: 2, x_lo: 2; x = x_hi * 2 + x_lo), y: 4, z: 4, core: 2. Of those that a mesh axis runs over, the one named last changes fastest.
Arguments:
- orbitals: float32 [16, 128, 128, 128], P('band', 'dom'), may hold values from -130 to 130
- potential: float32 [128, 128, 128], P('dom'), may hold values from -3 to 0
Outputs:
- ortho: float32 [16, 128, 128, 128], P('band', 'dom')
- correlation: float32 [16, 16], replicated
The draws below stay inside these ranges and needn't reach their ends.
All inputs are finite; a program needn't handle non-finite values.
Results may differ from the reference program's by a relative error of at most 0.00016.
Values sent between devices are 32-bit elements; how exact they have to be, the bound alone decides.
A program may use at most 192 MiB of HBM per device.

```python
import math
import jax
import jax.numpy as jnp
from jax import lax

GY = 128
GZ = 128
STEPS = 4
NS = 16
NX = 128


def draw_orbitals(key, part):
    key = jax.random.fold_in(key, 11)
    key_common, key_private = jax.random.split(key, 2)
    positions = jnp.arange(NX, dtype=jnp.float32)
    ramp_up = jnp.exp(math.log(10.0) * positions / max(NX - 1, 1)).reshape(1, NX, 1, 1)
    common = jnp.clip(jax.random.normal(key_common, (1, NX, GY, GZ), jnp.float32), -5.0, 5.0)
    private = jnp.clip(jax.random.normal(key_private, (NS, NX, GY, GZ), jnp.float32), -5.0, 5.0)
    values = (0.7 * common + private) * ramp_up
    return values.astype(jnp.float32)


def shard_levels(own_key, shape, pieces, least, largest):
    factor_of = 1.0
    for axis_at, blocks in pieces:
        steps = jax.random.uniform(jax.random.fold_in(jax.random.fold_in(own_key, 6), axis_at), (blocks,), jnp.float32, least / len(pieces), largest / len(pieces))
        factor_of = factor_of * jnp.repeat(jnp.exp(steps), shape[axis_at] // blocks).reshape((-1,) + (1,) * (len(shape) - 1 - axis_at))
    return factor_of


def setup_inputs(seed: int = 0) -> dict:
    key_list = jax.random.split(jax.random.key(seed), 3)
    return {
        "orbitals": draw_orbitals(jax.random.fold_in(key_list[2], 71), 0),
        "potential": jnp.clip(-3.0 + 3.0 * jax.random.uniform(key_list[1], (NX, GY, GZ), jnp.float32) ** shard_levels(key_list[1], (NX, GY, GZ), ((0, 8),), -0.2, 0.2), -3.0, 0.0),
    }


COEFFS = (-5369.0 / 1800.0, 12.0 / 7.0, -15.0 / 56.0, 10.0 / 189.0, -1.0 / 112.0, 2.0 / 1925.0, -1.0 / 16632.0)
LOWER_EDGE = -3.5
CUT_EDGE = 0.5
UPPER_EDGE = 11.0

def recurrence(count):
    half_width = (UPPER_EDGE - CUT_EDGE) / 2.0
    centre = (UPPER_EDGE + CUT_EDGE) / 2.0
    sigma_now = half_width / (LOWER_EDGE - centre)
    gamma_value = 2.0 / sigma_now
    plan = [(sigma_now / half_width, 0.0)]
    for number in range(count - 1):
        sigma_next = 1.0 / (gamma_value - sigma_now)
        plan.append((2.0 * sigma_next / half_width, sigma_now * sigma_next))
        sigma_now = sigma_next
    return (centre, plan)

def apply_hamiltonian(field_data, potential):
    laplace = 3.0 * COEFFS[0] * field_data
    for offset in range(1, 7):
        for axis_index in range(3):
            laplace = laplace + COEFFS[offset] * (jnp.roll(field_data, offset, axis_index) + jnp.roll(field_data, -offset, axis_index))
    return -0.5 * laplace + potential * field_data

def filter_one(initial, potential):
    centre, plan = recurrence(STEPS)
    current = initial
    previous = initial
    for scale_now, prev_weight in plan:
        applied = apply_hamiltonian(current, potential)
        updated = (applied - centre * current) * scale_now - prev_weight * previous
        previous = current
        current = updated
    return current

def reference(orbitals, potential):
    filtered = lax.map(lambda state_field: filter_one(state_field, potential), orbitals)
    flat_rows = filtered.reshape(NS, NX * GY * GZ)
    correlation = jnp.dot(flat_rows.astype(jnp.float32), flat_rows.T.astype(jnp.float32), precision=lax.Precision.HIGHEST, preferred_element_type=jnp.float32) / float(NX * GY * GZ)
    lower_factor = jnp.linalg.cholesky(correlation)
    ortho = jax.scipy.linalg.solve_triangular(lower_factor, flat_rows, lower=True)
    return (ortho.reshape(NS, NX, GY, GZ), correlation)
```

```python
import jax
import jax.numpy as jnp
from jax import lax
from jax.experimental import pallas as pl
from jax.experimental.pallas import tpu as pltpu
from jax.sharding import PartitionSpec as P

STEPS = 4
COEFFS = (
    -5369.0 / 1800.0,
    12.0 / 7.0,
    -15.0 / 56.0,
    10.0 / 189.0,
    -1.0 / 112.0,
    2.0 / 1925.0,
    -1.0 / 16632.0,
)
LOWER_EDGE = -3.5
CUT_EDGE = 0.5
UPPER_EDGE = 11.0
HALO = 6
MESH = pl.DeviceIdType.MESH
F32 = jnp.float32
BF16 = jnp.bfloat16


def recurrence(count):
    half_width = (UPPER_EDGE - CUT_EDGE) / 2.0
    centre = (UPPER_EDGE + CUT_EDGE) / 2.0
    sigma_now = half_width / (LOWER_EDGE - centre)
    gamma_value = 2.0 / sigma_now
    plan = [(sigma_now / half_width, 0.0)]
    for number in range(count - 1):
        sigma_next = 1.0 / (gamma_value - sigma_now)
        plan.append((2.0 * sigma_next / half_width, sigma_now * sigma_next))
        sigma_now = sigma_next
    return (centre, plan)


def halves(value):
    high = value.astype(BF16)
    return high, (value - high.astype(F32)).astype(BF16)


def circulant(size):
    row = lax.broadcasted_iota(jnp.int32, (size, size), 0)
    col = lax.broadcasted_iota(jnp.int32, (size, size), 1)
    gap = jnp.abs(row - col)
    gap = jnp.minimum(gap, size - gap)
    value = jnp.zeros((size, size), F32)
    for offset in range(1, HALO + 1):
        value = jnp.where(gap == offset, COEFFS[offset], value)
    return halves(value)


def kernel(nb, nd, x_in, v_in, out, corr, field, pot, wz, wy, recv, split, acc, ortho,
           ga, gb, s_x, r_x, s_v, r_v, s_o, r_o, s_i, r_i, s_f, r_f, s_a, r_a, s_b, r_b,
           s_r, r_r):
    planes, gy, gz = v_in.shape
    m = planes // nb
    edge = planes - HALO
    centre, plan = recurrence(STEPS)
    b, d = lax.axis_index("band"), lax.axis_index("dom")
    c, xl = lax.rem(b, 2), lax.rem(d, 2)
    xh = lax.rem(b // 2, 2)
    sid = b - c + xl
    e = d - xl + c

    def home(state, slab):
        sp, ep = lax.rem(state, 2), lax.rem(slab, 2)
        return (state - sp + ep, slab - ep + sp)

    e_out = lax.rem(e + 2 * c - 1 + nd, nd)
    e_in = e + 1 - 2 * c

    barrier = pltpu.get_barrier_semaphore()
    plane_group = nb * 2
    my_slot = b * 2 + xl

    @pl.loop(1, plane_group)
    def _(k):
        slot = lax.rem(my_slot + k, plane_group)
        pl.semaphore_signal(barrier, inc=1, device_id=(slot // 2, d - xl + lax.rem(slot, 2)),
                            device_id_type=MESH)

    @pl.loop(2, nd)
    def _(k):
        other = lax.rem(d - xl + k, nd)
        slab = other
        pl.semaphore_signal(barrier, inc=1, device_id=home(sid, slab), device_id_type=MESH)

    same = c == xl
    starts = (edge * c, edge * (1 - c), HALO)
    sizes = (HALO, HALO, planes - 2 * HALO)

    def local_x(j):
        return pltpu.make_async_copy(
            x_in.at[0, pl.ds(starts[j], sizes[j])],
            field.at[0, pl.ds(HALO + starts[j], sizes[j])], r_x.at[j])

    def local_v():
        return pltpu.make_async_copy(v_in, pot, r_v.at[0])

    @pl.when(same)
    def _():
        for j in range(3):
            local_x(j).start()
        local_v().start()

    high, low = circulant(gz)
    wz[0:gz, 0:gz] = high
    wz[gz:, 0:gz] = high
    wz[0:gz, gz:] = low
    wz[gz:, gz:] = jnp.zeros_like(low)
    high, low = circulant(gy)
    wy[0:gy, 0:gy] = high
    wy[0:gy, gy:] = high
    wy[gy:, 0:gy] = low
    wy[gy:, gy:] = jnp.zeros_like(low)

    pl.semaphore_wait(barrier, plane_group - 1 + nd - 2)

    back = (edge * xl, edge * (1 - xl), HALO)

    def swap(j):
        return pltpu.make_async_remote_copy(
            src_ref=x_in.at[0, pl.ds(back[j], sizes[j])],
            dst_ref=field.at[0, pl.ds(HALO + back[j], sizes[j])],
            send_sem=s_x.at[j], recv_sem=r_x.at[j], device_id=(sid, e), device_id_type=MESH)

    def give_v():
        return pltpu.make_async_remote_copy(
            src_ref=v_in, dst_ref=pot, send_sem=s_v.at[0], recv_sem=r_v.at[0],
            device_id=(b + 2 - 4 * xh, d + 1 - 2 * xl), device_id_type=MESH)

    @pl.when(jnp.logical_not(same))
    def _():
        for j in range(3):
            swap(j).start()

    @pl.when(same)
    def _():
        give_v().start()

    def outer_start(j):
        return edge * c + (1 - c) * (HALO - 2 - 2 * j) + c * 2 * j

    def send_outer(k, j):
        own = outer_start(j)
        there = own + HALO + planes + c * (-2 * planes)
        return pltpu.make_async_remote_copy(
            src_ref=field.at[k, pl.ds(HALO + own, 2)],
            dst_ref=field.at[k, pl.ds(there, 2)],
            send_sem=s_o.at[k, j], recv_sem=r_o.at[k, j],
            device_id=home(sid, e_out), device_id_type=MESH)

    def send_inner(k):
        return pltpu.make_async_remote_copy(
            src_ref=field.at[k, pl.ds(HALO + edge * (1 - c), HALO)],
            dst_ref=field.at[k, pl.ds((HALO + planes) * c, HALO)],
            send_sem=s_i.at[k], recv_sem=r_i.at[k],
            device_id=home(sid, e_in), device_id_type=MESH)

    local_x(0).wait()
    for j in range(3):
        send_outer(0, j).start()
    local_x(1).wait()
    send_inner(0).start()
    local_x(2).wait()
    local_v().wait()

    def pair(k, i, scale, weight):
        last = jnp.maximum(k - 2, 0)
        mid = field[k - 1, pl.ds(i + HALO, 2)]
        h0, l0 = halves(mid[0])
        h1, l1 = halves(mid[1])
        along_z = jnp.dot(
            jnp.concatenate([jnp.concatenate([h0, l0], 1), jnp.concatenate([h1, l1], 1)], 0),
            wz[...], preferred_element_type=F32)
        along_y = jnp.dot(
            wy[...],
            jnp.concatenate([jnp.concatenate([h0, h1], 1), jnp.concatenate([l0, l1], 1)], 0),
            preferred_element_type=F32)
        for t in range(2):
            off = (along_z[t * gy:(t + 1) * gy, 0:gz] + along_z[t * gy:(t + 1) * gy, gz:]
                   + along_y[0:gy, t * gz:(t + 1) * gz] + along_y[gy:, t * gz:(t + 1) * gz])
            for offset in range(1, HALO + 1):
                off = off + COEFFS[offset] * (
                    field[k - 1, i + HALO + t + offset] + field[k - 1, i + HALO + t - offset])
            here = mid[t]
            value = (pot[i + t] - (centre + 1.5 * COEFFS[0])) * here - 0.5 * off
            field[k, i + HALO + t] = value * scale - weight * field[last, i + HALO + t]

    @pl.loop(1, STEPS + 1)
    def _(k):
        scale, weight = F32(plan[0][0]), F32(plan[0][1])
        for step in range(1, STEPS):
            scale = jnp.where(k == step + 1, F32(plan[step][0]), scale)
            weight = jnp.where(k == step + 1, F32(plan[step][1]), weight)

        @pl.loop(0, (planes - 2 * HALO) // 2)
        def _(j):
            pair(k, HALO + 2 * j, scale, weight)

        send_inner(k - 1).wait_recv()

        @pl.loop(0, HALO // 2)
        def _(j):
            pair(k, edge * (1 - c) + 2 * j, scale, weight)

        @pl.when(k < STEPS)
        def _():
            send_inner(k).start()

        for j in range(HALO // 2):
            send_outer(k - 1, j).wait_recv()

        @pl.loop(0, HALO // 2)
        def _(j):
            pair(k, outer_start(j), scale, weight)

            @pl.when(k < STEPS)
            def _():
                send_outer(k, j).start()

    def spread(k):
        to = lax.rem(sid + k, nb)
        return pltpu.make_async_remote_copy(
            src_ref=field.at[STEPS, pl.ds(HALO + to * m, m)], dst_ref=recv.at[sid],
            send_sem=s_f.at[to], recv_sem=r_f.at[sid],
            device_id=home(to, e), device_id_type=MESH)

    def arrived(k):
        origin = lax.rem(sid + k, nb)
        return pltpu.make_async_copy(recv.at[origin], recv.at[origin], r_f.at[origin])

    @pl.loop(1, nb)
    def _(k):
        spread(k).start()

    recv[pl.ds(sid, 1)] = field[STEPS, pl.ds(HALO + sid * m, m)].reshape(1, m, gy, gz)

    @pl.loop(1, nb)
    def _(k):
        arrived(k).wait()

    rows = nb * 8
    groups = gy // 16
    acc[...] = jnp.zeros_like(acc)

    @pl.loop(0, m * groups)
    def _(g):
        mi, r0 = g // groups, lax.rem(g, groups) * 16
        r0 = pl.multiple_of(r0, 16)
        h0, l0 = halves(recv[:, mi, pl.ds(r0, 8), :].reshape(rows, gz))
        h1, l1 = halves(recv[:, mi, pl.ds(pl.multiple_of(r0 + 8, 8), 8), :].reshape(rows, gz))
        both = jnp.concatenate(
            [jnp.concatenate([h0, h1], 1), jnp.concatenate([l0, l1], 1)], 0)
        split[g] = both
        acc[...] += lax.dot_general(
            both, both, (((1,), (1,)), ((), ())), preferred_element_type=F32)

    total = acc[0:rows, 0:rows] + acc[0:rows, rows:] + acc[rows:, 0:rows] + acc[rows:, rows:]
    at_row = lax.broadcasted_iota(jnp.int32, (rows, rows), 0)
    at_col = lax.broadcasted_iota(jnp.int32, (rows, rows), 1)
    match = lax.rem(at_row, 8) == lax.rem(at_col, 8)
    total = jnp.where(match, total, 0.0).reshape(nb, 8, rows).sum(axis=1)
    fold_row = lax.broadcasted_iota(jnp.int32, (rows, 128), 0)
    fold_col = lax.broadcasted_iota(jnp.int32, (rows, 128), 1)
    fold = (fold_row // 8 == fold_col).astype(F32)
    ga[pl.ds(sid, 1)] = jnp.dot(
        total, fold, precision=lax.Precision.HIGHEST, preferred_element_type=F32)[None]

    def share_a(k):
        return pltpu.make_async_remote_copy(
            src_ref=ga.at[sid], dst_ref=ga.at[sid], send_sem=s_a.at[k], recv_sem=r_a.at[sid],
            device_id=home(lax.rem(sid + k, nb), e), device_id_type=MESH)

    def got_a(k):
        origin = lax.rem(sid + k, nb)
        return pltpu.make_async_copy(ga.at[origin], ga.at[origin], r_a.at[origin])

    @pl.loop(1, nb)
    def _(k):
        share_a(k).start()

    @pl.loop(1, nb)
    def _(k):
        got_a(k).wait()

    gb[pl.ds(e, 1)] = jnp.sum(ga[...], axis=0, keepdims=True)

    def share_b(k):
        return pltpu.make_async_remote_copy(
            src_ref=gb.at[e], dst_ref=gb.at[e], send_sem=s_b.at[k], recv_sem=r_b.at[e],
            device_id=home(sid, lax.rem(e + k, nd)), device_id_type=MESH)

    def got_b(k):
        origin = lax.rem(e + k, nd)
        return pltpu.make_async_copy(gb.at[origin], gb.at[origin], r_b.at[origin])

    @pl.loop(1, nd)
    def _(k):
        share_b(k).start()

    @pl.loop(1, nd)
    def _(k):
        got_b(k).wait()

    work = jnp.sum(gb[...], axis=0) / float(planes * nd * gy * gz)
    corr[...] = work[:, 0:nb]

    sub = lax.broadcasted_iota(jnp.int32, (nb, 128), 0)
    lane = lax.broadcasted_iota(jnp.int32, (nb, 128), 1)
    work = jnp.where(lane == sub + nb, 1.0, work)
    for k in range(nb - 1):
        factor = work[:, k:k + 1] / work[k:k + 1, k:k + 1]
        factor = jnp.where(sub > k, factor, 0.0)
        work = work - factor * work[k:k + 1, :]
    diagonal = jnp.sum(jnp.where(lane == sub, work, 0.0), axis=1, keepdims=True)
    work = work / jnp.sqrt(diagonal)

    wide_row = lax.broadcasted_iota(jnp.int32, (128, rows), 0)
    wide_col = lax.broadcasted_iota(jnp.int32, (128, rows), 1)
    widen = (wide_row == wide_col // 8 + nb).astype(F32)
    wide = jnp.dot(work, widen, precision=lax.Precision.HIGHEST, preferred_element_type=F32)
    wide = jnp.broadcast_to(wide[:, None, :], (nb, 8, rows)).reshape(rows, rows)
    high, low = halves(jnp.where(match, wide, 0.0))
    left = jnp.concatenate([high, low, high], 1)

    @pl.loop(0, m * groups)
    def _(g):
        mi, r0 = g // groups, lax.rem(g, groups) * 16
        r0 = pl.multiple_of(r0, 16)
        both = split[g]
        value = jnp.dot(left, jnp.concatenate([both[0:rows], both[0:rows], both[rows:]], 0),
                        preferred_element_type=F32)
        ortho[:, mi, pl.ds(r0, 8), :] = value[:, 0:gz].reshape(nb, 8, gz)
        ortho[:, mi, pl.ds(pl.multiple_of(r0 + 8, 8), 8), :] = value[:, gz:].reshape(nb, 8, gz)

    def give_back(k):
        state = lax.rem(b + k, nb)
        return pltpu.make_async_remote_copy(
            src_ref=ortho.at[state], dst_ref=out.at[0, pl.ds(sid * m, m)],
            send_sem=s_r.at[state], recv_sem=r_r.at[sid], device_id=(state, e),
            device_id_type=MESH)

    own_back = pltpu.make_async_copy(
        ortho.at[b], out.at[0, pl.ds(b * m, m)], r_r.at[b])

    @pl.loop(1, nb)
    def _(k):
        give_back(k).start()

    @pl.when(same)
    def _():
        own_back.start()

    @pl.when(jnp.logical_not(same))
    def _():
        give_back(0).start()

    @pl.loop(0, nb)
    def _(p):
        pltpu.make_async_copy(out.at[0, pl.ds(p * m, m)], out.at[0, pl.ds(p * m, m)],
                              r_r.at[p]).wait()

    @pl.when(jnp.logical_not(same))
    def _():
        for j in range(3):
            swap(j).wait_send()
        give_back(0).wait_send()

    @pl.when(same)
    def _():
        give_v().wait_send()

    @pl.loop(0, STEPS)
    def _(k):
        for j in range(HALO // 2):
            send_outer(k, j).wait_send()
        send_inner(k).wait_send()

    @pl.loop(1, nb)
    def _(k):
        spread(k).wait_send()
        share_a(k).wait_send()
        give_back(k).wait_send()

    @pl.loop(1, nd)
    def _(k):
        share_b(k).wait_send()


def shards(orbitals, potential):
    nb, nd = lax.axis_size("band"), lax.axis_size("dom")
    planes, gy, gz = potential.shape
    m = planes // nb
    rows = nb * 8
    dma = pltpu.SemaphoreType.DMA
    any_space = pl.BlockSpec(memory_space=pl.ANY)
    return pl.pallas_call(
        lambda *refs: kernel(nb, nd, *refs),
        out_shape=(jax.ShapeDtypeStruct(orbitals.shape, F32),
                   jax.ShapeDtypeStruct((nb, nb), F32)),
        in_specs=[any_space, any_space],
        out_specs=(any_space, pl.BlockSpec(memory_space=pltpu.VMEM)),
        scratch_shapes=[
            pltpu.VMEM((STEPS + 1, planes + 2 * HALO, gy, gz), F32),
            pltpu.VMEM((planes, gy, gz), F32),
            pltpu.VMEM((2 * gz, 2 * gz), BF16),
            pltpu.VMEM((2 * gy, 2 * gy), BF16),
            pltpu.VMEM((nb, m, gy, gz), F32),
            pltpu.VMEM((m * gy // 16, 2 * rows, 2 * gz), BF16),
            pltpu.VMEM((2 * rows, 2 * rows), F32),
            pltpu.VMEM((nb, m, gy, gz), F32),
            pltpu.VMEM((nb, nb, 128), F32),
            pltpu.VMEM((nd, nb, 128), F32),
            dma((3,)), dma((3,)),
            dma((1,)), dma((1,)),
            dma((STEPS, HALO // 2)), dma((STEPS, HALO // 2)),
            dma((STEPS,)), dma((STEPS,)),
            dma((nb,)), dma((nb,)),
            dma((nb,)), dma((nb,)),
            dma((nd,)), dma((nd,)),
            dma((nb,)), dma((nb,)),
        ],
        compiler_params=pltpu.CompilerParams(
            collective_id=0, has_side_effects=True, vmem_limit_bytes=40 * 1024 * 1024),
        cost_estimate=pl.CostEstimate(flops=2 * 10**9, bytes_accessed=4 * 10**6,
                                      transcendentals=0),
    )(orbitals, potential)


def solution(mesh):
    placed = (P("band", "dom", None, None), P("dom", None, None))
    return jax.shard_map(
        shards,
        mesh=mesh,
        in_specs=placed,
        out_specs=(P("band", "dom", None, None), P()),
        check_vma=False,
    )
```

```python
import jax
import jax.numpy as jnp
from jax import lax
from jax.experimental import pallas as pl
from jax.experimental.pallas import tpu as pltpu
from jax.sharding import PartitionSpec as P

STEPS = 4
COEFFS = (
    -5369.0 / 1800.0,
    12.0 / 7.0,
    -15.0 / 56.0,
    10.0 / 189.0,
    -1.0 / 112.0,
    2.0 / 1925.0,
    -1.0 / 16632.0,
)
LOWER_EDGE = -3.5
CUT_EDGE = 0.5
UPPER_EDGE = 11.0
HALO = 6
STRIPS = 4
MESH = pl.DeviceIdType.MESH
F32 = jnp.float32
BF16 = jnp.bfloat16


def recurrence(count):
    half_width = (UPPER_EDGE - CUT_EDGE) / 2.0
    centre = (UPPER_EDGE + CUT_EDGE) / 2.0
    sigma_now = half_width / (LOWER_EDGE - centre)
    gamma_value = 2.0 / sigma_now
    plan = [(sigma_now / half_width, 0.0)]
    for number in range(count - 1):
        sigma_next = 1.0 / (gamma_value - sigma_now)
        plan.append((2.0 * sigma_next / half_width, sigma_now * sigma_next))
        sigma_now = sigma_next
    return (centre, plan)


def halves(value):
    high = value.astype(BF16)
    return high, (value - high.astype(F32)).astype(BF16)


def circulant(size):
    row = lax.broadcasted_iota(jnp.int32, (size, size), 0)
    col = lax.broadcasted_iota(jnp.int32, (size, size), 1)
    gap = jnp.abs(row - col)
    gap = jnp.minimum(gap, size - gap)
    value = jnp.zeros((size, size), F32)
    for offset in range(1, HALO + 1):
        value = jnp.where(gap == offset, COEFFS[offset], value)
    return halves(value)


def kernel(nb, nd, x_in, v_in, out, corr, field, pot, wz, wy, recv, split, acc, ortho,
           ga, gb, s_x, r_x, s_v, r_v, s_o, r_o, s_i, r_i, s_f, r_f, s_a, r_a, s_b, r_b,
           s_r, r_r):
    planes, gy, gz = v_in.shape
    m = planes // nb
    edge = planes - HALO
    nz = nb // 4
    strip = gy // STRIPS
    centre, plan = recurrence(STEPS)
    b, d = lax.axis_index("band"), lax.axis_index("dom")
    c, xl = lax.rem(b, 2), lax.rem(d, 2)
    xh = lax.rem(b // 2, 2)
    z = b // 4
    x = 2 * xh + xl
    sid = b - c + xl
    e = d - xl + c
    same = c == xl
    apart = jnp.logical_not(same)

    def home(state, slab):
        sp, ep = lax.rem(state, 2), lax.rem(slab, 2)
        return (state - sp + ep, slab - ep + sp)

    e_out = lax.rem(e + 2 * c - 1 + nd, nd)
    e_in = e + 1 - 2 * c

    around = [(kz, kx) for kz in range(nz) for kx in range(4) if kz or kx]
    around.sort(key=lambda k: -min(k[0], nz - k[0]) - min(k[1], 4 - k[1]))

    def toward(kz, kx):
        return lax.rem(z + kz, nz) * 4 + lax.rem(x + kx, 4)

    barrier = pltpu.get_barrier_semaphore()
    plane_group = nb * 2
    my_slot = b * 2 + xl

    @pl.loop(1, plane_group)
    def _(k):
        slot = lax.rem(my_slot + k, plane_group)
        pl.semaphore_signal(barrier, inc=1, device_id=(slot // 2, d - xl + lax.rem(slot, 2)),
                            device_id_type=MESH)

    @pl.loop(2, nd)
    def _(k):
        pl.semaphore_signal(barrier, inc=1, device_id=home(sid, lax.rem(d - xl + k, nd)),
                            device_id_type=MESH)

    def part(j, side):
        if j < STRIPS:
            return pl.ds(edge * side, HALO), pl.ds(j * strip, strip)
        if j == STRIPS:
            return pl.ds(HALO + (edge - 2 * HALO) * side, HALO), pl.ds(0, gy)
        return pl.ds(2 * HALO * (1 - side), planes - 2 * HALO), pl.ds(0, gy)

    def part_v(j, side):
        if j == 0:
            return pl.ds(edge * side, HALO)
        return pl.ds(HALO * (1 - side), edge)

    def shifted(rows):
        return pl.ds(HALO + rows.start, rows.size)

    def local_x(j):
        at, rows = part(j, c)
        return pltpu.make_async_copy(x_in.at[0, at, rows], field.at[0, shifted(at), rows],
                                     r_x.at[j])

    def local_v(j):
        at = part_v(j, c)
        return pltpu.make_async_copy(v_in.at[at], pot.at[at], r_v.at[j])

    @pl.when(same)
    def _():
        for j in range(STRIPS + 2):
            local_x(j).start()
        for j in range(2):
            local_v(j).start()

    high, low = circulant(gz)
    wz[0:gz, 0:gz] = high
    wz[gz:, 0:gz] = high
    wz[0:gz, gz:] = low
    wz[gz:, gz:] = jnp.zeros_like(low)
    high, low = circulant(gy)
    wy[0:gy, 0:gy] = high
    wy[0:gy, gy:] = high
    wy[gy:, 0:gy] = low
    wy[gy:, gy:] = jnp.zeros_like(low)

    pl.semaphore_wait(barrier, plane_group - 1 + nd - 2)

    def swap(j):
        at, rows = part(j, xl)
        return pltpu.make_async_remote_copy(
            src_ref=x_in.at[0, at, rows], dst_ref=field.at[0, shifted(at), rows],
            send_sem=s_x.at[j], recv_sem=r_x.at[j], device_id=(sid, e), device_id_type=MESH)

    def give_v(j):
        at = part_v(j, c)
        return pltpu.make_async_remote_copy(
            src_ref=v_in.at[at], dst_ref=pot.at[at], send_sem=s_v.at[j], recv_sem=r_v.at[j],
            device_id=(b + 2 - 4 * xh, d + 1 - 2 * xl), device_id_type=MESH)

    @pl.when(apart)
    def _():
        for j in range(STRIPS + 2):
            swap(j).start()

    @pl.when(same)
    def _():
        for j in range(2):
            give_v(j).start()

    def send_outer(k, j):
        rows = pl.ds(j * strip, strip)
        return pltpu.make_async_remote_copy(
            src_ref=field.at[k, pl.ds(HALO + edge * c, HALO), rows],
            dst_ref=field.at[k, pl.ds((HALO + planes) * (1 - c), HALO), rows],
            send_sem=s_o.at[k, j], recv_sem=r_o.at[k, j],
            device_id=home(sid, e_out), device_id_type=MESH)

    def send_inner(k):
        return pltpu.make_async_remote_copy(
            src_ref=field.at[k, pl.ds(HALO + edge * (1 - c), HALO)],
            dst_ref=field.at[k, pl.ds((HALO + planes) * c, HALO)],
            send_sem=s_i.at[k], recv_sem=r_i.at[k],
            device_id=home(sid, e_in), device_id_type=MESH)

    def own(rank):
        return rank + c * (planes - 1 - 2 * rank)

    def pair(k, rank, inside):
        scale, weight = plan[k - 1]
        mid = [field[k - 1, HALO + own(rank + t)] for t in range(2)]
        h0, l0 = halves(mid[0])
        h1, l1 = halves(mid[1])
        along_z = jnp.dot(
            jnp.concatenate([jnp.concatenate([h0, l0], 1), jnp.concatenate([h1, l1], 1)], 0),
            wz[...], preferred_element_type=F32)
        along_y = jnp.dot(
            wy[...],
            jnp.concatenate([jnp.concatenate([h0, h1], 1), jnp.concatenate([l0, l1], 1)], 0),
            preferred_element_type=F32)
        for t in range(2):
            here = rank + t
            off = (along_z[t * gy:(t + 1) * gy, 0:gz] + along_z[t * gy:(t + 1) * gy, gz:]
                   + along_y[0:gy, t * gz:(t + 1) * gz] + along_y[gy:, t * gz:(t + 1) * gz])
            for offset in range(1, HALO + 1):
                far = field[k - 1, HALO + own(here + offset)]
                if inside or here >= offset:
                    far = far + field[k - 1, HALO + own(here - offset)]
                off = off + COEFFS[offset] * far
            value = (pot[own(here)] - (centre + 1.5 * COEFFS[0])) * mid[t] - 0.5 * off
            value = value * scale
            if k > 1:
                value = value - weight * field[k - 2, HALO + own(here)]
            field[k, HALO + own(here)] = value

    def before_halo(k):
        for rank in range(0, HALO, 2):
            pair(k, rank, False)

    def with_halo(k, j):
        rows = pl.ds(j * strip, strip)
        send_outer(k - 1, j).wait_recv()
        for rank in range(HALO):
            off = COEFFS[rank + 1] * field[k - 1, HALO + own(-1), rows]
            for offset in range(rank + 2, HALO + 1):
                off = off + COEFFS[offset] * field[k - 1, HALO + own(rank - offset), rows]
            at = HALO + own(rank)
            field[k, at, rows] = field[k, at, rows] - (0.5 * plan[k - 1][0]) * off
        if k < STEPS:
            send_outer(k, j).start()

    def middle(k):
        @pl.loop(0, (planes - 2 * HALO) // 2)
        def _(j):
            pair(k, HALO + 2 * j, True)

    def inner(k):
        send_inner(k - 1).wait_recv()

        @pl.loop(0, HALO // 2)
        def _(j):
            pair(k, edge + 2 * j, True)

        if k < STEPS:
            send_inner(k).start()

    for j in range(STRIPS):
        local_x(j).wait()
        send_outer(0, j).start()
    local_x(STRIPS).wait()
    local_v(0).wait()
    before_halo(1)
    for j in range(STRIPS):
        with_halo(1, j)
    local_x(STRIPS + 1).wait()
    send_inner(0).start()
    local_v(1).wait()
    middle(1)
    inner(1)

    for k in range(2, STEPS):
        before_halo(k)
        with_halo(k, 0)
        middle(k)
        with_halo(k, 1)
        inner(k)
        for j in range(2, STRIPS):
            with_halo(k, j)

    late = -(-HALO // m)
    half = gy // 2

    def is_late(part_at):
        return jnp.where(c == 0, part_at < late, part_at >= nb - late)

    def spread(kz, kx, rows, j):
        to = toward(kz, kx)
        return pltpu.make_async_remote_copy(
            src_ref=field.at[STEPS, pl.ds(HALO + to * m, m), rows],
            dst_ref=recv.at[sid, pl.ds(0, m), rows],
            send_sem=s_f.at[to, j], recv_sem=r_f.at[sid, j],
            device_id=home(to, e), device_id_type=MESH)

    def arrived(kz, kx, rows, j):
        origin = toward(kz, kx)
        at = recv.at[origin, pl.ds(0, m), rows]
        return pltpu.make_async_copy(at, at, r_f.at[origin, j])

    first, second, whole = pl.ds(0, half), pl.ds(half, half), pl.ds(0, gy)

    before_halo(STEPS)
    middle(STEPS)
    inner(STEPS)
    for kz, kx in around:
        @pl.when(jnp.logical_not(is_late(toward(kz, kx))))
        def _():
            spread(kz, kx, whole, 0).start()
    for j in range(STRIPS // 2):
        with_halo(STEPS, j)
    for kz, kx in around:
        @pl.when(is_late(toward(kz, kx)))
        def _():
            spread(kz, kx, first, 0).start()
    for j in range(STRIPS // 2, STRIPS):
        with_halo(STEPS, j)
    for kz, kx in around:
        @pl.when(is_late(toward(kz, kx)))
        def _():
            spread(kz, kx, second, 1).start()
    recv[pl.ds(sid, 1)] = field[STEPS, pl.ds(HALO + sid * m, m)].reshape(1, m, gy, gz)

    rows = nb * 8
    groups = gy // 16
    acc[...] = jnp.zeros_like(acc)
    mine_late = is_late(sid)

    def products(g0):
        @pl.loop(0, m * groups // 2)
        def _(g):
            mi, r0 = g // (groups // 2), (lax.rem(g, groups // 2) + g0) * 16
            r0 = pl.multiple_of(r0, 16)
            h0, l0 = halves(recv[:, mi, pl.ds(r0, 8), :].reshape(rows, gz))
            h1, l1 = halves(
                recv[:, mi, pl.ds(pl.multiple_of(r0 + 8, 8), 8), :].reshape(rows, gz))
            both = jnp.concatenate(
                [jnp.concatenate([h0, h1], 1), jnp.concatenate([l0, l1], 1)], 0)
            split[mi * groups + g0 + lax.rem(g, groups // 2)] = both
            acc[...] += lax.dot_general(
                both, both, (((1,), (1,)), ((), ())), preferred_element_type=F32)

    @pl.when(mine_late)
    def _():
        for kz, kx in around:
            arrived(kz, kx, first, 0).wait()

    @pl.when(jnp.logical_not(mine_late))
    def _():
        for kz, kx in around:
            arrived(kz, kx, whole, 0).wait()

    products(0)

    @pl.when(mine_late)
    def _():
        for kz, kx in around:
            arrived(kz, kx, second, 1).wait()

    products(groups // 2)

    total = acc[0:rows, 0:rows] + acc[0:rows, rows:] + acc[rows:, 0:rows] + acc[rows:, rows:]
    at_row = lax.broadcasted_iota(jnp.int32, (rows, rows), 0)
    at_col = lax.broadcasted_iota(jnp.int32, (rows, rows), 1)
    match = lax.rem(at_row, 8) == lax.rem(at_col, 8)
    total = jnp.where(match, total, 0.0).reshape(nb, 8, rows).sum(axis=1)
    fold_row = lax.broadcasted_iota(jnp.int32, (rows, 128), 0)
    fold_col = lax.broadcasted_iota(jnp.int32, (rows, 128), 1)
    fold = (fold_row // 8 == fold_col).astype(F32)
    ga[pl.ds(sid, 1)] = jnp.dot(
        total, fold, precision=lax.Precision.HIGHEST, preferred_element_type=F32)[None]

    def share_a(kz, kx):
        to = toward(kz, kx)
        return pltpu.make_async_remote_copy(
            src_ref=ga.at[sid], dst_ref=ga.at[sid], send_sem=s_a.at[to], recv_sem=r_a.at[sid],
            device_id=home(to, e), device_id_type=MESH)

    def got_a(kz, kx):
        origin = toward(kz, kx)
        return pltpu.make_async_copy(ga.at[origin], ga.at[origin], r_a.at[origin])

    for kz, kx in around:
        share_a(kz, kx).start()
    for kz, kx in around:
        got_a(kz, kx).wait()

    gb[pl.ds(e, 1)] = jnp.sum(ga[...], axis=0, keepdims=True)

    def share_b(k):
        to = lax.rem(e + k, nd)
        return pltpu.make_async_remote_copy(
            src_ref=gb.at[e], dst_ref=gb.at[e], send_sem=s_b.at[k], recv_sem=r_b.at[e],
            device_id=home(sid, to), device_id_type=MESH)

    def got_b(k):
        origin = lax.rem(e + k, nd)
        return pltpu.make_async_copy(gb.at[origin], gb.at[origin], r_b.at[origin])

    for k in range(1, nd):
        share_b(k).start()
    for k in range(1, nd):
        got_b(k).wait()

    work = jnp.sum(gb[...], axis=0) / float(planes * nd * gy * gz)
    corr[...] = work[:, 0:nb]

    sub = lax.broadcasted_iota(jnp.int32, (nb, 128), 0)
    lane = lax.broadcasted_iota(jnp.int32, (nb, 128), 1)
    work = jnp.where(lane == sub + nb, 1.0, work)
    for k in range(nb - 1):
        factor = work[:, k:k + 1] / work[k:k + 1, k:k + 1]
        factor = jnp.where(sub > k, factor, 0.0)
        work = work - factor * work[k:k + 1, :]
    diagonal = jnp.sum(jnp.where(lane == sub, work, 0.0), axis=1, keepdims=True)
    work = work / jnp.sqrt(diagonal)

    wide_row = lax.broadcasted_iota(jnp.int32, (128, rows), 0)
    wide_col = lax.broadcasted_iota(jnp.int32, (128, rows), 1)
    widen = (wide_row == wide_col // 8 + nb).astype(F32)
    wide = jnp.dot(work, widen, precision=lax.Precision.HIGHEST, preferred_element_type=F32)
    wide = jnp.broadcast_to(wide[:, None, :], (nb, 8, rows)).reshape(rows, rows)
    high, low = halves(jnp.where(match, wide, 0.0))
    left = jnp.concatenate([high, low, high], 1)

    @pl.loop(0, m * groups)
    def _(g):
        mi, r0 = g // groups, lax.rem(g, groups) * 16
        r0 = pl.multiple_of(r0, 16)
        both = split[g]
        value = jnp.dot(left, jnp.concatenate([both[0:rows], both[0:rows], both[rows:]], 0),
                        preferred_element_type=F32)
        ortho[:, mi, pl.ds(r0, 8), :] = value[:, 0:gz].reshape(nb, 8, gz)
        ortho[:, mi, pl.ds(pl.multiple_of(r0 + 8, 8), 8), :] = value[:, gz:].reshape(nb, 8, gz)

    back = [(kz, h, t) for kz in range(nz) for h in range(2) for t in range(2)]
    back.sort(key=lambda k: (-min(k[0], nz - k[0]) - k[1], -k[2]))

    def give_back(kz, h, t):
        column = lax.rem(xh + h + jnp.where(jnp.logical_and(apart, xl == 1), 1, 0), 2)
        state = lax.rem(z + kz, nz) * 4 + column * 2 + lax.rem(c + t, 2)
        return pltpu.make_async_remote_copy(
            src_ref=ortho.at[state], dst_ref=out.at[0, pl.ds(sid * m, m)],
            send_sem=s_r.at[state], recv_sem=r_r.at[sid], device_id=(state, e),
            device_id_type=MESH)

    own_back = pltpu.make_async_copy(
        ortho.at[b], out.at[0, pl.ds(b * m, m)], r_r.at[b])

    for item in back[:-1]:
        give_back(*item).start()

    @pl.when(same)
    def _():
        own_back.start()

    @pl.when(apart)
    def _():
        give_back(*back[-1]).start()

    @pl.loop(0, nb)
    def _(p):
        pltpu.make_async_copy(out.at[0, pl.ds(p * m, m)], out.at[0, pl.ds(p * m, m)],
                              r_r.at[p]).wait()

    @pl.when(apart)
    def _():
        for j in range(STRIPS + 2):
            swap(j).wait_send()
        give_back(*back[-1]).wait_send()

    @pl.when(same)
    def _():
        for j in range(2):
            give_v(j).wait_send()

    for k in range(STEPS):
        for j in range(STRIPS):
            send_outer(k, j).wait_send()
        send_inner(k).wait_send()

    for kz, kx in around:
        @pl.when(is_late(toward(kz, kx)))
        def _():
            spread(kz, kx, first, 0).wait_send()
            spread(kz, kx, second, 1).wait_send()

        @pl.when(jnp.logical_not(is_late(toward(kz, kx))))
        def _():
            spread(kz, kx, whole, 0).wait_send()

        share_a(kz, kx).wait_send()

    for k in range(1, nd):
        share_b(k).wait_send()
    for item in back[:-1]:
        give_back(*item).wait_send()


def shards(orbitals, potential):
    nb, nd = lax.axis_size("band"), lax.axis_size("dom")
    planes, gy, gz = potential.shape
    m = planes // nb
    rows = nb * 8
    dma = pltpu.SemaphoreType.DMA
    any_space = pl.BlockSpec(memory_space=pl.ANY)
    hbm = pl.BlockSpec(memory_space=pltpu.HBM)
    return pl.pallas_call(
        lambda *refs: kernel(nb, nd, *refs),
        out_shape=(jax.ShapeDtypeStruct(orbitals.shape, F32),
                   jax.ShapeDtypeStruct((nb, nb), F32)),
        in_specs=[hbm, hbm],
        out_specs=(any_space, pl.BlockSpec(memory_space=pltpu.VMEM)),
        scratch_shapes=[
            pltpu.VMEM((STEPS + 1, planes + 2 * HALO, gy, gz), F32),
            pltpu.VMEM((planes, gy, gz), F32),
            pltpu.VMEM((2 * gz, 2 * gz), BF16),
            pltpu.VMEM((2 * gy, 2 * gy), BF16),
            pltpu.VMEM((nb, m, gy, gz), F32),
            pltpu.VMEM((m * gy // 16, 2 * rows, 2 * gz), BF16),
            pltpu.VMEM((2 * rows, 2 * rows), F32),
            pltpu.VMEM((nb, m, gy, gz), F32),
            pltpu.VMEM((nb, nb, 128), F32),
            pltpu.VMEM((nd, nb, 128), F32),
            dma((STRIPS + 2,)), dma((STRIPS + 2,)),
            dma((2,)), dma((2,)),
            dma((STEPS, STRIPS)), dma((STEPS, STRIPS)),
            dma((STEPS,)), dma((STEPS,)),
            dma((nb, 2)), dma((nb, 2)),
            dma((nb,)), dma((nb,)),
            dma((nd,)), dma((nd,)),
            dma((nb,)), dma((nb,)),
        ],
        compiler_params=pltpu.CompilerParams(
            collective_id=0, has_side_effects=True, vmem_limit_bytes=40 * 1024 * 1024),
        cost_estimate=pl.CostEstimate(flops=2 * 10**9, bytes_accessed=4 * 10**6,
                                      transcendentals=0),
    )(orbitals, potential)


def solution(mesh):
    placed = (P("band", "dom", None, None), P("dom", None, None))
    return jax.shard_map(
        shards,
        mesh=mesh,
        in_specs=placed,
        out_specs=(P("band", "dom", None, None), P()),
        check_vma=False,
    )
```

```python
import jax
import jax.numpy as jnp
from jax import lax
from jax.experimental import pallas as pl
from jax.experimental.pallas import tpu as pltpu
from jax.sharding import PartitionSpec as P

STEPS = 4
COEFFS = (
    -5369.0 / 1800.0,
    12.0 / 7.0,
    -15.0 / 56.0,
    10.0 / 189.0,
    -1.0 / 112.0,
    2.0 / 1925.0,
    -1.0 / 16632.0,
)
LOWER_EDGE = -3.5
CUT_EDGE = 0.5
UPPER_EDGE = 11.0
HALO = 6
STRIPS = 4
EARLY = 4
MESH = pl.DeviceIdType.MESH
F32 = jnp.float32
BF16 = jnp.bfloat16


def recurrence(count):
    half_width = (UPPER_EDGE - CUT_EDGE) / 2.0
    centre = (UPPER_EDGE + CUT_EDGE) / 2.0
    sigma_now = half_width / (LOWER_EDGE - centre)
    gamma_value = 2.0 / sigma_now
    plan = [(sigma_now / half_width, 0.0)]
    for number in range(count - 1):
        sigma_next = 1.0 / (gamma_value - sigma_now)
        plan.append((2.0 * sigma_next / half_width, sigma_now * sigma_next))
        sigma_now = sigma_next
    return (centre, plan)


def halves(value):
    high = value.astype(BF16)
    return high, (value - high.astype(F32)).astype(BF16)


def circulant(size):
    row = lax.broadcasted_iota(jnp.int32, (size, size), 0)
    col = lax.broadcasted_iota(jnp.int32, (size, size), 1)
    gap = jnp.abs(row - col)
    gap = jnp.minimum(gap, size - gap)
    value = jnp.zeros((size, size), F32)
    for offset in range(1, HALO + 1):
        value = jnp.where(gap == offset, COEFFS[offset], value)
    return halves(value)


def kernel(nb, nd, x_in, v_in, out, corr, field, pot, wz, wy, t_out, t_in, recv, split, ortho,
           ga, gb, s_x, r_x, s_v, r_v, s_o, r_o, s_i, r_i, s_f, r_f, s_a, r_a, s_b, r_b,
           s_r, r_r):
    planes, gy, gz = v_in.shape
    edge = planes - HALO
    nz, ny = nb // 4, nd // 2
    strip = gy // STRIPS
    half = gy // 2
    centre, plan = recurrence(STEPS)
    b, d = lax.axis_index("band"), lax.axis_index("dom")
    c, xl = lax.rem(b, 2), lax.rem(d, 2)
    xh = lax.rem(b // 2, 2)
    y, z = d // 2, b // 4
    x = 2 * xh + xl
    sid = b - c + xl
    e = d - xl + c
    same = c == xl
    apart = jnp.logical_not(same)

    def home(state, slab):
        sp, ep = lax.rem(state, 2), lax.rem(slab, 2)
        return (state - sp + ep, slab - ep + sp)

    e_out = lax.rem(e + 2 * c - 1 + nd, nd)
    e_in = e + 1 - 2 * c

    def way(k, n):
        return min(k, n - k)

    around = [(kz, kx) for kz in range(nz) for kx in range(4) if kz or kx]
    around.sort(key=lambda k: -way(k[0], nz) - way(k[1], 4))
    column = [(ky, kc) for ky in range(ny) for kc in range(2) if ky or kc]
    column.sort(key=lambda k: -2 * way(k[0], ny) - k[1])

    def state_at(kz, kx):
        return lax.rem(z + kz, nz) * 4 + lax.rem(x + kx, 4)

    def slab_at(ky, kc):
        return lax.rem(y + ky, ny) * 2 + lax.rem(c + kc, 2)

    barrier = pltpu.get_barrier_semaphore()
    for kz, kx in around:
        for kc in range(2):
            pl.semaphore_signal(barrier, inc=1, device_id=home(state_at(kz, kx), slab_at(0, kc)),
                                device_id_type=MESH)
    for ky, kc in column:
        pl.semaphore_signal(barrier, inc=1, device_id=home(sid, slab_at(ky, kc)),
                            device_id_type=MESH)
    greeted = 2 * len(around) + len(column)

    def part(j, side):
        if j < STRIPS:
            return pl.ds(edge * side, HALO), pl.ds(j * strip, strip)
        if j == STRIPS:
            return pl.ds(HALO + (edge - 2 * HALO) * side, HALO), pl.ds(0, gy)
        return pl.ds(2 * HALO * (1 - side), planes - 2 * HALO), pl.ds(0, gy)

    def part_v(j, side):
        if j == 0:
            return pl.ds(edge * side, HALO)
        return pl.ds(HALO * (1 - side), edge)

    def shifted(rows):
        return pl.ds(HALO + rows.start, rows.size)

    def local_x(j):
        at, rows = part(j, c)
        return pltpu.make_async_copy(x_in.at[0, at, rows], field.at[0, shifted(at), rows],
                                     r_x.at[j])

    def local_v(j):
        at = part_v(j, c)
        return pltpu.make_async_copy(v_in.at[at], pot.at[at], r_v.at[j])

    @pl.when(same)
    def _():
        for j in range(STRIPS + 2):
            local_x(j).start()
        for j in range(2):
            local_v(j).start()

    high, low = circulant(gz)
    wz[0:gz, 0:gz] = high
    wz[gz:, 0:gz] = high
    wz[0:gz, gz:] = low
    wz[gz:, gz:] = jnp.zeros_like(low)
    high, low = circulant(gy)
    wy[0:gy, 0:gy] = high
    wy[0:gy, gy:] = high
    wy[gy:, 0:gy] = low
    wy[gy:, gy:] = jnp.zeros_like(low)

    pl.semaphore_wait(barrier, greeted)

    def swap(j):
        at, rows = part(j, xl)
        return pltpu.make_async_remote_copy(
            src_ref=x_in.at[0, at, rows], dst_ref=field.at[0, shifted(at), rows],
            send_sem=s_x.at[j], recv_sem=r_x.at[j], device_id=(sid, e), device_id_type=MESH)

    def give_v(j):
        at = part_v(j, c)
        return pltpu.make_async_remote_copy(
            src_ref=v_in.at[at], dst_ref=pot.at[at], send_sem=s_v.at[j], recv_sem=r_v.at[j],
            device_id=(b + 2 - 4 * xh, d + 1 - 2 * xl), device_id_type=MESH)

    @pl.when(apart)
    def _():
        for j in range(STRIPS + 2):
            swap(j).start()

    @pl.when(same)
    def _():
        for j in range(2):
            give_v(j).start()

    def send_outer(k, j):
        rows = pl.ds(j * strip, strip)
        return pltpu.make_async_remote_copy(
            src_ref=field.at[k, pl.ds(HALO + edge * c, HALO), rows],
            dst_ref=field.at[k, pl.ds((HALO + planes) * (1 - c), HALO), rows],
            send_sem=s_o.at[k, j], recv_sem=r_o.at[k, j],
            device_id=home(sid, e_out), device_id_type=MESH)

    def send_inner(k):
        return pltpu.make_async_remote_copy(
            src_ref=field.at[k, pl.ds(HALO + edge * (1 - c), HALO)],
            dst_ref=field.at[k, pl.ds((HALO + planes) * c, HALO)],
            send_sem=s_i.at[k], recv_sem=r_i.at[k],
            device_id=home(sid, e_in), device_id_type=MESH)

    def own(rank):
        return rank + c * (planes - 1 - 2 * rank)

    def turned(k, rank, n, terms):
        high, low = [], []
        for t in range(n):
            h, l = halves(field[k - 1, HALO + own(rank + t)])
            high.append(h)
            low.append(l)
        along_z = jnp.dot(
            jnp.concatenate([jnp.concatenate([h, l], 1) for h, l in zip(high, low)], 0),
            wz[...], preferred_element_type=F32)
        along_y = jnp.dot(
            wy[...], jnp.concatenate([jnp.concatenate(high, 1), jnp.concatenate(low, 1)], 0),
            preferred_element_type=F32)
        for t in range(n):
            terms[t] = (along_z[t * gy:(t + 1) * gy, 0:gz] + along_z[t * gy:(t + 1) * gy, gz:]
                        + along_y[0:gy, t * gz:(t + 1) * gz] + along_y[gy:, t * gz:(t + 1) * gz])

    def planes_of(k, rank, n, terms):
        scale, weight = plan[k - 1]
        shift = -(centre + 1.5 * COEFFS[0]) * scale
        factor = -0.5 * scale
        for r0 in range(0, gy, 16):
            rows = pl.ds(r0, 16)
            first = rank - HALO if rank else 0
            near = {j: field[k - 1, HALO + own(j), rows] for j in range(first, rank + n + HALO)}
            for t in range(n):
                here = rank + t
                value = (pot[own(here), rows] * scale + shift) * near[here]
                value = value + factor * terms[t, rows]
                for offset in range(1, HALO + 1):
                    side = near[here + offset]
                    if here - offset in near:
                        side = side + near[here - offset]
                    value = value + (factor * COEFFS[offset]) * side
                if k > 1:
                    value = value - weight * field[k - 2, HALO + own(here), rows]
                field[k, HALO + own(here), rows] = value

    def with_halo(k, j):
        factor = -0.5 * plan[k - 1][0]
        send_outer(k - 1, j).wait_recv()
        for r0 in range(0, strip, 16):
            rows = pl.ds(j * strip + r0, min(16, strip))
            near = [field[k - 1, HALO + own(-offset), rows] for offset in range(1, HALO + 1)]
            for rank in range(HALO):
                at = HALO + own(rank)
                value = field[k, at, rows]
                for offset in range(rank + 1, HALO + 1):
                    value = value + (factor * COEFFS[offset]) * near[offset - rank - 1]
                field[k, at, rows] = value
        if k < STEPS:
            send_outer(k, j).start()

    body = planes - 2 * HALO
    t_mid, t_inner = t_in.at[pl.ds(0, body)], t_in.at[pl.ds(body, HALO)]

    def outer(k):
        turned(k, 0, HALO, t_out)
        planes_of(k, 0, HALO, t_out)

    def turn_inner(k):
        turned(k, HALO, body, t_mid)
        turned(k, edge, HALO, t_inner)

    first, second, whole = pl.ds(0, half), pl.ds(half, half), pl.ds(0, gy)

    def spread(to, rows, j):
        return pltpu.make_async_remote_copy(
            src_ref=field.at[STEPS, HALO + to, rows], dst_ref=recv.at[sid, rows],
            send_sem=s_f.at[to, j], recv_sem=r_f.at[sid, j],
            device_id=home(to, e), device_id_type=MESH)

    def spread_ranks(rank, n, rows, j, act):
        for k in range(n):
            to = own(rank + lax.rem(k + z + x, n))

            @pl.when(to != sid)
            def _():
                act(spread(to, rows, j))

    def start(copy):
        copy.start()

    def wait_send(copy):
        copy.wait_send()

    for j in range(STRIPS):
        local_x(j).wait()
        send_outer(0, j).start()
    local_x(STRIPS).wait()
    local_v(0).wait()
    outer(1)
    for j in range(STRIPS):
        with_halo(1, j)
    local_x(STRIPS + 1).wait()
    send_inner(0).start()
    turn_inner(1)
    local_v(1).wait()
    planes_of(1, HALO, body, t_mid)
    send_inner(0).wait_recv()
    planes_of(1, edge, HALO, t_inner)
    send_inner(1).start()
    turn_inner(2)

    for k in range(2, STEPS):
        outer(k)
        with_halo(k, 0)
        planes_of(k, HALO, body, t_mid)
        with_halo(k, 1)
        send_inner(k - 1).wait_recv()
        planes_of(k, edge, HALO, t_inner)
        send_inner(k).start()
        for j in range(2, STRIPS - 1):
            with_halo(k, j)
        turn_inner(k + 1)
        if k < STEPS - 1:
            with_halo(k, STRIPS - 1)

    deep = HALO - EARLY
    send_inner(STEPS - 1).wait_recv()
    planes_of(STEPS, planes - EARLY, EARLY, t_inner.at[pl.ds(deep, EARLY)])
    spread_ranks(planes - EARLY, EARLY, whole, 0, start)
    with_halo(STEPS - 1, STRIPS - 1)
    planes_of(STEPS, HALO, body + deep, t_in.at[pl.ds(0, body + deep)])
    spread_ranks(HALO, body + deep, whole, 0, start)
    outer(STEPS)
    for j in range(STRIPS // 2):
        with_halo(STEPS, j)
    spread_ranks(0, HALO, first, 0, start)
    for j in range(STRIPS // 2, STRIPS):
        with_halo(STEPS, j)
    spread_ranks(0, HALO, second, 1, start)
    recv[pl.ds(sid, 1)] = field[STEPS, pl.ds(HALO + sid, 1)]

    tall = nb * 8
    wide = half // 8 * gz
    late = jnp.where(c == 0, sid < HALO, sid >= edge)

    def arrived(rows, j):
        for kz, kx in around:
            at = recv.at[state_at(kz, kx), rows]
            pltpu.make_async_copy(at, at, r_f.at[state_at(kz, kx), j]).wait()

    def products(j):
        high, low = [], []
        for g in range(half // 8):
            h, l = halves(recv[:, j * half + 8 * g:j * half + 8 * g + 8, :].reshape(tall, gz))
            high.append(h)
            low.append(l)
        both = jnp.concatenate([jnp.concatenate(high, 1), jnp.concatenate(low, 1)], 0)
        split[:, j * wide:(j + 1) * wide] = both
        return lax.dot_general(both, both, (((1,), (1,)), ((), ())), preferred_element_type=F32)

    @pl.when(late)
    def _():
        arrived(first, 0)

    @pl.when(jnp.logical_not(late))
    def _():
        arrived(whole, 0)

    total = products(0)

    @pl.when(late)
    def _():
        arrived(second, 1)

    total = total + products(1)
    total = total[0:tall, 0:tall] + total[0:tall, tall:] + total[tall:, 0:tall] + total[tall:, tall:]
    at_row = lax.broadcasted_iota(jnp.int32, (tall, tall), 0)
    at_col = lax.broadcasted_iota(jnp.int32, (tall, tall), 1)
    match = lax.rem(at_row, 8) == lax.rem(at_col, 8)
    gb[pl.ds(e, 1)] = jnp.where(match, total, 0.0).reshape(nb, 8, tall).sum(axis=1)[None]

    def share_b(ky, kc):
        to = slab_at(ky, kc)
        return pltpu.make_async_remote_copy(
            src_ref=gb.at[e], dst_ref=gb.at[e], send_sem=s_b.at[to], recv_sem=r_b.at[e],
            device_id=home(sid, to), device_id_type=MESH)

    for ky, kc in column:
        share_b(ky, kc).start()
    for ky, kc in reversed(column):
        origin = slab_at(ky, kc)
        pltpu.make_async_copy(gb.at[origin], gb.at[origin], r_b.at[origin]).wait()
    ga[pl.ds(sid, 1)] = jnp.sum(gb[...], axis=0, keepdims=True)

    def share_a(kz, kx):
        to = state_at(kz, kx)
        return pltpu.make_async_remote_copy(
            src_ref=ga.at[sid], dst_ref=ga.at[sid], send_sem=s_a.at[to], recv_sem=r_a.at[sid],
            device_id=home(to, e), device_id_type=MESH)

    for kz, kx in around:
        share_a(kz, kx).start()
    same_state = (at_row // 8 == at_col // 8).astype(F32)
    for kz, kx in reversed(around):
        origin = state_at(kz, kx)
        pltpu.make_async_copy(ga.at[origin], ga.at[origin], r_a.at[origin]).wait()

    whole_sum = jnp.sum(ga[...], axis=0) / float(planes * nd * gy * gz)
    matrix = jnp.dot(whole_sum, same_state, precision=lax.Precision.HIGHEST,
                     preferred_element_type=F32)

    sub = lax.broadcasted_iota(jnp.int32, (nb, tall), 0)
    lane = lax.broadcasted_iota(jnp.int32, (nb, tall), 1)
    work = matrix
    inverse = (sub == lane // 8).astype(F32)
    for k in range(nb - 1):
        factor = work[:, 8 * k:8 * k + 1] / work[k:k + 1, 8 * k:8 * k + 1]
        factor = jnp.where(sub > k, factor, 0.0)
        work = work - factor * work[k:k + 1, :]
        inverse = inverse - factor * inverse[k:k + 1, :]
    diagonal = jnp.sum(jnp.where(lane == 8 * sub, work, 0.0), axis=1, keepdims=True)
    inverse = inverse / jnp.sqrt(diagonal)

    inverse = jnp.broadcast_to(inverse[:, None, :], (nb, 8, tall)).reshape(tall, tall)
    high, low = halves(jnp.where(match, inverse, 0.0))
    left = jnp.concatenate([jnp.concatenate([high, high], 1),
                            jnp.concatenate([low, jnp.zeros_like(low)], 1)], 0)

    back = [(kz, h, t) for kz in range(nz) for h in range(2) for t in range(2)]
    back.sort(key=lambda k: (-way(k[0], nz) - k[1], -k[2]))

    def give_back(kz, h, t, j):
        state = lax.rem(z + kz, nz) * 4 + lax.rem(xh + h, 2) * 2 + lax.rem(c + t, 2)
        rows = (first, second)[j]
        return pltpu.make_async_remote_copy(
            src_ref=ortho.at[state, rows], dst_ref=out.at[0, sid, rows],
            send_sem=s_r.at[state, j], recv_sem=r_r.at[sid, j], device_id=(state, e),
            device_id_type=MESH)

    def own_back(j):
        rows = (first, second)[j]
        return pltpu.make_async_copy(ortho.at[b, rows], out.at[0, b, rows], r_r.at[b, j])

    for j in range(2):
        value = jnp.dot(left, split[:, j * wide:(j + 1) * wide], preferred_element_type=F32)
        for g in range(half // 8):
            at = slice(g * gz, (g + 1) * gz)
            ortho[:, j * half + 8 * g:j * half + 8 * g + 8, :] = (
                value[0:tall, at] + value[tall:, at]).reshape(nb, 8, gz)
        for item in back[:-1]:
            give_back(*item, j).start()

        @pl.when(same)
        def _():
            own_back(j).start()

        @pl.when(apart)
        def _():
            give_back(*back[-1], j).start()

    pick_row = lax.broadcasted_iota(jnp.int32, (tall, nb), 0)
    pick_col = lax.broadcasted_iota(jnp.int32, (tall, nb), 1)
    corr[...] = jnp.dot(matrix, (pick_row == 8 * pick_col).astype(F32),
                        precision=lax.Precision.HIGHEST, preferred_element_type=F32)

    @pl.when(apart)
    def _():
        for j in range(STRIPS + 2):
            swap(j).wait_send()

    @pl.when(same)
    def _():
        for j in range(2):
            give_v(j).wait_send()

    for k in range(STEPS):
        for j in range(STRIPS):
            send_outer(k, j).wait_send()
        send_inner(k).wait_send()
    spread_ranks(HALO, edge, whole, 0, wait_send)
    spread_ranks(0, HALO, first, 0, wait_send)
    spread_ranks(0, HALO, second, 1, wait_send)
    for ky, kc in column:
        share_b(ky, kc).wait_send()
    for kz, kx in around:
        share_a(kz, kx).wait_send()

    for j in range(2):
        for item in back[:-1]:
            give_back(*item, j).wait_send()

        @pl.when(apart)
        def _():
            give_back(*back[-1], j).wait_send()

        @pl.loop(0, nb)
        def _(p):
            at = out.at[0, p, (first, second)[j]]
            pltpu.make_async_copy(at, at, r_r.at[p, j]).wait()


def shards(orbitals, potential):
    nb, nd = lax.axis_size("band"), lax.axis_size("dom")
    planes, gy, gz = potential.shape
    tall = nb * 8
    dma = pltpu.SemaphoreType.DMA
    any_space = pl.BlockSpec(memory_space=pl.ANY)
    hbm = pl.BlockSpec(memory_space=pltpu.HBM)
    return pl.pallas_call(
        lambda *refs: kernel(nb, nd, *refs),
        out_shape=(jax.ShapeDtypeStruct(orbitals.shape, F32),
                   jax.ShapeDtypeStruct((nb, nb), F32)),
        in_specs=[hbm, hbm],
        out_specs=(any_space, pl.BlockSpec(memory_space=pltpu.VMEM)),
        scratch_shapes=[
            pltpu.VMEM((STEPS + 1, planes + 2 * HALO, gy, gz), F32),
            pltpu.VMEM((planes, gy, gz), F32),
            pltpu.VMEM((2 * gz, 2 * gz), BF16),
            pltpu.VMEM((2 * gy, 2 * gy), BF16),
            pltpu.VMEM((HALO, gy, gz), F32),
            pltpu.VMEM((planes - HALO, gy, gz), F32),
            pltpu.VMEM((nb, gy, gz), F32),
            pltpu.VMEM((2 * tall, gy // 8 * gz), BF16),
            pltpu.VMEM((nb, gy, gz), F32),
            pltpu.VMEM((nb, nb, tall), F32),
            pltpu.VMEM((nd, nb, tall), F32),
            dma((STRIPS + 2,)), dma((STRIPS + 2,)),
            dma((2,)), dma((2,)),
            dma((STEPS, STRIPS)), dma((STEPS, STRIPS)),
            dma((STEPS,)), dma((STEPS,)),
            dma((nb, 2)), dma((nb, 2)),
            dma((nb,)), dma((nb,)),
            dma((nd,)), dma((nd,)),
            dma((nb, 2)), dma((nb, 2)),
        ],
        compiler_params=pltpu.CompilerParams(
            collective_id=0, has_side_effects=True, vmem_limit_bytes=60 * 1024 * 1024),
        cost_estimate=pl.CostEstimate(flops=2 * 10**9, bytes_accessed=4 * 10**6,
                                      transcendentals=0),
    )(orbitals, potential)


def solution(mesh):
    placed = (P("band", "dom", None, None), P("dom", None, None))
    return jax.shard_map(
        shards,
        mesh=mesh,
        in_specs=placed,
        out_specs=(P("band", "dom", None, None), P()),
        check_vma=False,
    )
```

```python
import jax
import jax.numpy as jnp
from jax import lax
from jax.experimental import pallas as pl
from jax.experimental.pallas import tpu as pltpu
from jax.sharding import PartitionSpec as P

STEPS = 4
COEFFS = (
    -5369.0 / 1800.0,
    12.0 / 7.0,
    -15.0 / 56.0,
    10.0 / 189.0,
    -1.0 / 112.0,
    2.0 / 1925.0,
    -1.0 / 16632.0,
)
LOWER_EDGE = -3.5
CUT_EDGE = 0.5
UPPER_EDGE = 11.0
HALO = 6
STRIPS = 4
EARLY = 4
MESH = pl.DeviceIdType.MESH
F32 = jnp.float32
BF16 = jnp.bfloat16


def recurrence(count):
    half_width = (UPPER_EDGE - CUT_EDGE) / 2.0
    centre = (UPPER_EDGE + CUT_EDGE) / 2.0
    sigma_now = half_width / (LOWER_EDGE - centre)
    gamma_value = 2.0 / sigma_now
    plan = [(sigma_now / half_width, 0.0)]
    for number in range(count - 1):
        sigma_next = 1.0 / (gamma_value - sigma_now)
        plan.append((2.0 * sigma_next / half_width, sigma_now * sigma_next))
        sigma_now = sigma_next
    return (centre, plan)


def halves(value):
    high = value.astype(BF16)
    return high, (value - high.astype(F32)).astype(BF16)


def circulant(size):
    row = lax.broadcasted_iota(jnp.int32, (size, size), 0)
    col = lax.broadcasted_iota(jnp.int32, (size, size), 1)
    gap = jnp.abs(row - col)
    gap = jnp.minimum(gap, size - gap)
    value = jnp.zeros((size, size), F32)
    for offset in range(1, HALO + 1):
        value = jnp.where(gap == offset, COEFFS[offset], value)
    return halves(value)


def kernel(nb, nd, x_in, v_in, out, corr, scale, field, pot, wz, wy, t_out, t_in, recv, split, ortho,
           ga, gb, s_x, r_x, s_v, r_v, s_o, r_o, s_i, r_i, s_f, r_f, s_a, r_a, s_b, r_b,
           s_r, r_r):
    planes, gy, gz = v_in.shape
    edge = planes - HALO
    nz, ny = nb // 4, nd // 2
    strip = gy // STRIPS
    half = gy // 2
    centre, plan = recurrence(STEPS)
    b, d = lax.axis_index("band"), lax.axis_index("dom")
    c, xl = lax.rem(b, 2), lax.rem(d, 2)
    xh = lax.rem(b // 2, 2)
    y, z = d // 2, b // 4
    x = 2 * xh + xl
    sid = b - c + xl
    e = d - xl + c
    same = c == xl
    apart = jnp.logical_not(same)

    def home(state, slab):
        sp, ep = lax.rem(state, 2), lax.rem(slab, 2)
        return (state - sp + ep, slab - ep + sp)

    e_out = lax.rem(e + 2 * c - 1 + nd, nd)
    e_in = e + 1 - 2 * c

    def way(k, n):
        return min(k, n - k)

    around = [(kz, kx) for kz in range(nz) for kx in range(4) if kz or kx]
    around.sort(key=lambda k: -way(k[0], nz) - way(k[1], 4))
    column = [(ky, kc) for ky in range(ny) for kc in range(2) if ky or kc]
    column.sort(key=lambda k: -2 * way(k[0], ny) - k[1])

    def state_at(kz, kx):
        return lax.rem(z + kz, nz) * 4 + lax.rem(x + kx, 4)

    def slab_at(ky, kc):
        return lax.rem(y + ky, ny) * 2 + lax.rem(c + kc, 2)

    barrier = pltpu.get_barrier_semaphore()
    for kz, kx in around:
        for kc in range(2):
            pl.semaphore_signal(barrier, inc=1, device_id=home(state_at(kz, kx), slab_at(0, kc)),
                                device_id_type=MESH)
    for ky, kc in column:
        pl.semaphore_signal(barrier, inc=1, device_id=home(sid, slab_at(ky, kc)),
                            device_id_type=MESH)
    greeted = 2 * len(around) + len(column)

    def part(j, side):
        if j < STRIPS:
            return pl.ds(edge * side, HALO), pl.ds(j * strip, strip)
        if j == STRIPS:
            return pl.ds(HALO + (edge - 2 * HALO) * side, HALO), pl.ds(0, gy)
        return pl.ds(2 * HALO * (1 - side), planes - 2 * HALO), pl.ds(0, gy)

    def part_v(j, side):
        if j == 0:
            return pl.ds(edge * side, HALO)
        return pl.ds(HALO * (1 - side), edge)

    def shifted(rows):
        return pl.ds(HALO + rows.start, rows.size)

    def local_x(j):
        at, rows = part(j, c)
        return pltpu.make_async_copy(x_in.at[0, at, rows], field.at[0, shifted(at), rows],
                                     r_x.at[j])

    def local_v(j):
        at = part_v(j, c)
        return pltpu.make_async_copy(v_in.at[at], pot.at[at], r_v.at[j])

    @pl.when(same)
    def _():
        for j in range(STRIPS + 2):
            local_x(j).start()
        for j in range(2):
            local_v(j).start()

    pl.semaphore_wait(barrier, greeted)

    def swap(j):
        at, rows = part(j, xl)
        return pltpu.make_async_remote_copy(
            src_ref=x_in.at[0, at, rows], dst_ref=field.at[0, shifted(at), rows],
            send_sem=s_x.at[j], recv_sem=r_x.at[j], device_id=(sid, e), device_id_type=MESH)

    def give_v(j):
        at = part_v(j, c)
        return pltpu.make_async_remote_copy(
            src_ref=v_in.at[at], dst_ref=pot.at[at], send_sem=s_v.at[j], recv_sem=r_v.at[j],
            device_id=(b + 2 - 4 * xh, d + 1 - 2 * xl), device_id_type=MESH)

    @pl.when(apart)
    def _():
        for j in range(STRIPS + 2):
            swap(j).start()

    @pl.when(same)
    def _():
        for j in range(2):
            give_v(j).start()

    high, low = circulant(gz)
    wz[0:gz, 0:gz] = high
    wz[gz:, 0:gz] = high
    wz[0:gz, gz:] = low
    wz[gz:, gz:] = jnp.zeros_like(low)
    high, low = circulant(gy)
    wy[0:gy, 0:gy] = high
    wy[0:gy, gy:] = high
    wy[gy:, 0:gy] = low
    wy[gy:, gy:] = jnp.zeros_like(low)

    def send_outer(k, j):
        rows = pl.ds(j * strip, strip)
        return pltpu.make_async_remote_copy(
            src_ref=field.at[k, pl.ds(HALO + edge * c, HALO), rows],
            dst_ref=field.at[k, pl.ds((HALO + planes) * (1 - c), HALO), rows],
            send_sem=s_o.at[k, j], recv_sem=r_o.at[k, j],
            device_id=home(sid, e_out), device_id_type=MESH)

    def send_inner(k):
        return pltpu.make_async_remote_copy(
            src_ref=field.at[k, pl.ds(HALO + edge * (1 - c), HALO)],
            dst_ref=field.at[k, pl.ds((HALO + planes) * c, HALO)],
            send_sem=s_i.at[k], recv_sem=r_i.at[k],
            device_id=home(sid, e_in), device_id_type=MESH)

    def own(rank):
        return rank + c * (planes - 1 - 2 * rank)

    def turned(k, rank, n, terms):
        high, low = [], []
        for t in range(n):
            h, l = halves(field[k - 1, HALO + own(rank + t)])
            high.append(h)
            low.append(l)
        along_z = jnp.dot(
            jnp.concatenate([jnp.concatenate([h, l], 1) for h, l in zip(high, low)], 0),
            wz[...], preferred_element_type=F32)
        along_y = jnp.dot(
            wy[...], jnp.concatenate([jnp.concatenate(high, 1), jnp.concatenate(low, 1)], 0),
            preferred_element_type=F32)
        for t in range(n):
            terms[t] = (along_z[t * gy:(t + 1) * gy, 0:gz] + along_z[t * gy:(t + 1) * gy, gz:]
                        + along_y[0:gy, t * gz:(t + 1) * gz] + along_y[gy:, t * gz:(t + 1) * gz])

    def planes_of(k, rank, n, terms, top=0, bottom=None):
        step_weight, weight = plan[k - 1]
        shift = -(centre + 1.5 * COEFFS[0]) * step_weight
        factor = -0.5 * step_weight
        for r0 in range(top, gy if bottom is None else bottom, 16):
            rows = pl.ds(r0, min(16, strip))
            first = rank - HALO if rank else 0
            near = {j: field[k - 1, HALO + own(j), rows] for j in range(first, rank + n + HALO)}
            for t in range(n):
                here = rank + t
                value = (pot[own(here), rows] * step_weight + shift) * near[here]
                value = value + factor * terms[t, rows]
                for offset in range(1, HALO + 1):
                    side = near[here + offset]
                    if here - offset in near:
                        side = side + near[here - offset]
                    value = value + (factor * COEFFS[offset]) * side
                if k > 1:
                    value = value - weight * field[k - 2, HALO + own(here), rows]
                field[k, HALO + own(here), rows] = value

    def with_halo(k, j):
        factor = -0.5 * plan[k - 1][0]
        planes_of(k, 0, HALO, t_out, j * strip, (j + 1) * strip)
        send_outer(k - 1, j).wait_recv()
        for r0 in range(0, strip, 16):
            rows = pl.ds(j * strip + r0, min(16, strip))
            near = [field[k - 1, HALO + own(-offset), rows] for offset in range(1, HALO + 1)]
            for rank in range(HALO):
                at = HALO + own(rank)
                value = field[k, at, rows]
                for offset in range(rank + 1, HALO + 1):
                    value = value + (factor * COEFFS[offset]) * near[offset - rank - 1]
                field[k, at, rows] = value
        if k < STEPS:
            send_outer(k, j).start()

    body = planes - 2 * HALO
    t_mid, t_inner = t_in.at[pl.ds(0, body)], t_in.at[pl.ds(body, HALO)]

    def turn_outer(k):
        turned(k, 0, HALO, t_out)

    def turn_inner(k):
        turned(k, HALO, body, t_mid)
        turned(k, edge, HALO, t_inner)

    first, second, whole = pl.ds(0, half), pl.ds(half, half), pl.ds(0, gy)

    def spread(to, rows, j):
        return pltpu.make_async_remote_copy(
            src_ref=field.at[STEPS, HALO + to, rows], dst_ref=recv.at[sid, rows],
            send_sem=s_f.at[to, j], recv_sem=r_f.at[sid, j],
            device_id=home(to, e), device_id_type=MESH)

    def spread_ranks(rank, n, rows, j, act):
        for k in range(n):
            to = own(rank + lax.rem(k + z + x, n))

            @pl.when(to != sid)
            def _():
                act(spread(to, rows, j))

    def start(copy):
        copy.start()

    def wait_send(copy):
        copy.wait_send()

    for j in range(STRIPS):
        local_x(j).wait()
        send_outer(0, j).start()
    turn_outer(1)
    local_v(0).wait()
    local_x(STRIPS).wait()
    for j in range(STRIPS):
        with_halo(1, j)
    local_x(STRIPS + 1).wait()
    send_inner(0).start()
    turn_inner(1)
    local_v(1).wait()
    planes_of(1, HALO, body, t_mid)
    send_inner(0).wait_recv()
    planes_of(1, edge, HALO, t_inner)
    send_inner(1).start()

    for k in range(2, STEPS):
        turn_outer(k)
        with_halo(k, 0)
        turn_inner(k)
        planes_of(k, HALO, body, t_mid)
        with_halo(k, 1)
        send_inner(k - 1).wait_recv()
        planes_of(k, edge, HALO, t_inner)
        send_inner(k).start()
        for j in range(2, STRIPS - 1):
            with_halo(k, j)
        if k < STEPS - 1:
            with_halo(k, STRIPS - 1)
    turn_inner(STEPS)

    deep = HALO - EARLY
    send_inner(STEPS - 1).wait_recv()
    planes_of(STEPS, planes - EARLY, EARLY, t_inner.at[pl.ds(deep, EARLY)])
    spread_ranks(planes - EARLY, EARLY, whole, 0, start)
    with_halo(STEPS - 1, STRIPS - 1)
    planes_of(STEPS, HALO, body + deep, t_in.at[pl.ds(0, body + deep)])
    spread_ranks(HALO, body + deep, whole, 0, start)
    turn_outer(STEPS)
    for j in range(STRIPS // 2):
        with_halo(STEPS, j)
    spread_ranks(0, HALO, first, 0, start)
    for j in range(STRIPS // 2, STRIPS):
        with_halo(STEPS, j)
    spread_ranks(0, HALO, second, 1, start)
    recv[pl.ds(sid, 1)] = field[STEPS, pl.ds(HALO + sid, 1)]

    tall = nb * 8
    wide = half // 8 * gz
    late = jnp.where(c == 0, sid < HALO, sid >= edge)

    def arrived(rows, j):
        for kz, kx in around:
            at = recv.at[state_at(kz, kx), rows]
            pltpu.make_async_copy(at, at, r_f.at[state_at(kz, kx), j]).wait()

    def products(j):
        high, low = [], []
        for g in range(half // 8):
            h, l = halves(recv[:, j * half + 8 * g:j * half + 8 * g + 8, :].reshape(tall, gz))
            high.append(h)
            low.append(l)
        both = jnp.concatenate([jnp.concatenate(high, 1), jnp.concatenate(low, 1)], 0)
        split[:, j * wide:(j + 1) * wide] = both
        return lax.dot_general(both, both, (((1,), (1,)), ((), ())), preferred_element_type=F32)

    @pl.when(late)
    def _():
        arrived(first, 0)

    @pl.when(jnp.logical_not(late))
    def _():
        arrived(whole, 0)

    total = products(0)

    @pl.when(late)
    def _():
        arrived(second, 1)

    total = total + products(1)
    total = total[0:tall, 0:tall] + total[0:tall, tall:] + total[tall:, 0:tall] + total[tall:, tall:]
    at_row = lax.broadcasted_iota(jnp.int32, (tall, tall), 0)
    at_col = lax.broadcasted_iota(jnp.int32, (tall, tall), 1)
    match = lax.rem(at_row, 8) == lax.rem(at_col, 8)
    gb[pl.ds(e, 1)] = jnp.where(match, total, 0.0).reshape(nb, 8, tall).sum(axis=1)[None]

    def share_b(ky, kc):
        to = slab_at(ky, kc)
        return pltpu.make_async_remote_copy(
            src_ref=gb.at[e], dst_ref=gb.at[e], send_sem=s_b.at[to], recv_sem=r_b.at[e],
            device_id=home(sid, to), device_id_type=MESH)

    for ky, kc in column:
        share_b(ky, kc).start()
    for ky, kc in reversed(column):
        origin = slab_at(ky, kc)
        pltpu.make_async_copy(gb.at[origin], gb.at[origin], r_b.at[origin]).wait()
    ga[pl.ds(sid, 1)] = jnp.sum(gb[...], axis=0, keepdims=True)

    def share_a(kz, kx):
        to = state_at(kz, kx)
        return pltpu.make_async_remote_copy(
            src_ref=ga.at[sid], dst_ref=ga.at[sid], send_sem=s_a.at[to], recv_sem=r_a.at[sid],
            device_id=home(to, e), device_id_type=MESH)

    for kz, kx in around:
        share_a(kz, kx).start()
    same_state = (at_row // 8 == at_col // 8).astype(F32)
    for kz, kx in reversed(around):
        origin = state_at(kz, kx)
        pltpu.make_async_copy(ga.at[origin], ga.at[origin], r_a.at[origin]).wait()

    whole_sum = jnp.sum(ga[...], axis=0) / float(planes * nd * gy * gz)
    matrix = jnp.dot(whole_sum, same_state, precision=lax.Precision.HIGHEST,
                     preferred_element_type=F32)

    sub = lax.broadcasted_iota(jnp.int32, (nb, tall), 0)
    lane = lax.broadcasted_iota(jnp.int32, (nb, tall), 1)
    work = matrix
    inverse = (sub == lane // 8).astype(F32)
    for k in range(nb - 1):
        factor = work[:, 8 * k:8 * k + 1] / work[k:k + 1, 8 * k:8 * k + 1]
        factor = jnp.where(sub > k, factor, 0.0)
        work = work - factor * work[k:k + 1, :]
        inverse = inverse - factor * inverse[k:k + 1, :]
    diagonal = jnp.sum(jnp.where(lane == 8 * sub, work, 0.0), axis=1, keepdims=True)

    inverse = jnp.broadcast_to(inverse[:, None, :], (nb, 8, tall)).reshape(tall, tall)
    high, low = halves(jnp.where(match, inverse, 0.0))
    left = jnp.concatenate([jnp.concatenate([high, high], 1),
                            jnp.concatenate([low, jnp.zeros_like(low)], 1)], 0)

    back = [(kz, h, t) for kz in range(nz) for h in range(2) for t in range(2)]
    back.sort(key=lambda k: (-way(k[0], nz) - k[1], -k[2]))

    def give_back(kz, h, t, j):
        state = lax.rem(z + kz, nz) * 4 + lax.rem(xh + h, 2) * 2 + lax.rem(c + t, 2)
        rows = (first, second)[j]
        return pltpu.make_async_remote_copy(
            src_ref=ortho.at[state, rows], dst_ref=out.at[0, sid, rows],
            send_sem=s_r.at[state, j], recv_sem=r_r.at[sid, j], device_id=(state, e),
            device_id_type=MESH)

    def own_back(j):
        rows = (first, second)[j]
        return pltpu.make_async_copy(ortho.at[b, rows], out.at[0, b, rows], r_r.at[b, j])

    for j in range(2):
        value = jnp.dot(left, split[:, j * wide:(j + 1) * wide], preferred_element_type=F32)
        for g in range(half // 8):
            at = slice(g * gz, (g + 1) * gz)
            ortho[:, j * half + 8 * g:j * half + 8 * g + 8, :] = (
                value[0:tall, at] + value[tall:, at]).reshape(nb, 8, gz)
        for item in back[:-1]:
            give_back(*item, j).start()

        @pl.when(same)
        def _():
            own_back(j).start()

        @pl.when(apart)
        def _():
            give_back(*back[-1], j).start()

    pick = jnp.logical_and(at_row == 8 * at_col, at_col < nb).astype(F32)
    packed = jnp.dot(matrix, pick, precision=lax.Precision.HIGHEST, preferred_element_type=F32)
    corr[...] = packed[:, 0:nb]
    own_scale = jnp.sum(jnp.where(sub == b, 1.0 / jnp.sqrt(diagonal), 0.0), axis=0, keepdims=True)
    scale[...] = jnp.broadcast_to(own_scale, (1, tall))

    @pl.when(apart)
    def _():
        for j in range(STRIPS + 2):
            swap(j).wait_send()

    @pl.when(same)
    def _():
        for j in range(2):
            give_v(j).wait_send()

    for k in range(STEPS):
        for j in range(STRIPS):
            send_outer(k, j).wait_send()
        send_inner(k).wait_send()
    spread_ranks(HALO, edge, whole, 0, wait_send)
    spread_ranks(0, HALO, first, 0, wait_send)
    spread_ranks(0, HALO, second, 1, wait_send)
    for ky, kc in column:
        share_b(ky, kc).wait_send()
    for kz, kx in around:
        share_a(kz, kx).wait_send()

    for j in range(2):
        for item in back[:-1]:
            give_back(*item, j).wait_send()

        @pl.when(apart)
        def _():
            give_back(*back[-1], j).wait_send()

        @pl.loop(0, nb)
        def _(p):
            at = out.at[0, p, (first, second)[j]]
            pltpu.make_async_copy(at, at, r_r.at[p, j]).wait()


def shards(orbitals, potential):
    nb, nd = lax.axis_size("band"), lax.axis_size("dom")
    planes, gy, gz = potential.shape
    tall = nb * 8
    dma = pltpu.SemaphoreType.DMA
    any_space = pl.BlockSpec(memory_space=pl.ANY)
    hbm = pl.BlockSpec(memory_space=pltpu.HBM)
    rough, correlation, scale = pl.pallas_call(
        lambda *refs: kernel(nb, nd, *refs),
        out_shape=(jax.ShapeDtypeStruct(orbitals.shape, F32),
                   jax.ShapeDtypeStruct((nb, nb), F32),
                   jax.ShapeDtypeStruct((1, tall), F32)),
        in_specs=[hbm, hbm],
        out_specs=(any_space,) + (pl.BlockSpec(memory_space=pltpu.VMEM),) * 2,
        scratch_shapes=[
            pltpu.VMEM((STEPS + 1, planes + 2 * HALO, gy, gz), F32),
            pltpu.VMEM((planes, gy, gz), F32),
            pltpu.VMEM((2 * gz, 2 * gz), BF16),
            pltpu.VMEM((2 * gy, 2 * gy), BF16),
            pltpu.VMEM((HALO, gy, gz), F32),
            pltpu.VMEM((planes - HALO, gy, gz), F32),
            pltpu.VMEM((nb, gy, gz), F32),
            pltpu.VMEM((2 * tall, gy // 8 * gz), BF16),
            pltpu.VMEM((nb, gy, gz), F32),
            pltpu.VMEM((nb, nb, tall), F32),
            pltpu.VMEM((nd, nb, tall), F32),
            dma((STRIPS + 2,)), dma((STRIPS + 2,)),
            dma((2,)), dma((2,)),
            dma((STEPS, STRIPS)), dma((STEPS, STRIPS)),
            dma((STEPS,)), dma((STEPS,)),
            dma((nb, 2)), dma((nb, 2)),
            dma((nb,)), dma((nb,)),
            dma((nd,)), dma((nd,)),
            dma((nb, 2)), dma((nb, 2)),
        ],
        compiler_params=pltpu.CompilerParams(
            collective_id=0, has_side_effects=True, vmem_limit_bytes=60 * 1024 * 1024),
        cost_estimate=pl.CostEstimate(flops=2 * 10**9, bytes_accessed=4 * 10**6,
                                      transcendentals=0),
    )(orbitals, potential)
    return rough * scale, correlation


def solution(mesh):
    placed = (P("band", "dom", None, None), P("dom", None, None))
    return jax.shard_map(
        shards,
        mesh=mesh,
        in_specs=placed,
        out_specs=(P("band", "dom", None, None), P()),
        check_vma=False,
    )
```

```python
import jax
import jax.numpy as jnp
from jax import lax
from jax.experimental import pallas as pl
from jax.experimental.pallas import tpu as pltpu
from jax.sharding import PartitionSpec as P

STEPS = 4
COEFFS = (
    -5369.0 / 1800.0,
    12.0 / 7.0,
    -15.0 / 56.0,
    10.0 / 189.0,
    -1.0 / 112.0,
    2.0 / 1925.0,
    -1.0 / 16632.0,
)
LOWER_EDGE = -3.5
CUT_EDGE = 0.5
UPPER_EDGE = 11.0
HALO = 6
STRIPS = 4
EARLY = 4
MESH = pl.DeviceIdType.MESH
F32 = jnp.float32
BF16 = jnp.bfloat16


def recurrence(count):
    half_width = (UPPER_EDGE - CUT_EDGE) / 2.0
    centre = (UPPER_EDGE + CUT_EDGE) / 2.0
    sigma_now = half_width / (LOWER_EDGE - centre)
    gamma_value = 2.0 / sigma_now
    plan = [(sigma_now / half_width, 0.0)]
    for number in range(count - 1):
        sigma_next = 1.0 / (gamma_value - sigma_now)
        plan.append((2.0 * sigma_next / half_width, sigma_now * sigma_next))
        sigma_now = sigma_next
    return (centre, plan)


def halves(value):
    high = value.astype(BF16)
    return high, (value - high.astype(F32)).astype(BF16)


def circulant(size):
    row = lax.broadcasted_iota(jnp.int32, (size, size), 0)
    col = lax.broadcasted_iota(jnp.int32, (size, size), 1)
    gap = jnp.abs(row - col)
    gap = jnp.minimum(gap, size - gap)
    value = jnp.zeros((size, size), F32)
    for offset in range(1, HALO + 1):
        value = jnp.where(gap == offset, COEFFS[offset], value)
    return halves(value)


def kernel(nb, nd, x_in, v_in, out, corr, field, pot, wz, wy, t_out, t_in, recv, split, ortho,
           ga, gb, s_x, r_x, s_v, r_v, s_o, r_o, s_i, r_i, s_f, r_f, s_a, r_a, s_b, r_b,
           s_r, r_r):
    planes, gy, gz = v_in.shape
    edge = planes - HALO
    nz, ny = nb // 4, nd // 2
    strip = gy // STRIPS
    half = gy // 2
    centre, plan = recurrence(STEPS)
    b, d = lax.axis_index("band"), lax.axis_index("dom")
    c, xl = lax.rem(b, 2), lax.rem(d, 2)
    xh = lax.rem(b // 2, 2)
    y, z = d // 2, b // 4
    x = 2 * xh + xl
    sid = b - c + xl
    e = d - xl + c
    same = c == xl
    apart = jnp.logical_not(same)

    def home(state, slab):
        sp, ep = lax.rem(state, 2), lax.rem(slab, 2)
        return (state - sp + ep, slab - ep + sp)

    e_out = lax.rem(e + 2 * c - 1 + nd, nd)
    e_in = e + 1 - 2 * c

    def way(k, n):
        return min(k, n - k)

    around = [(kz, kx) for kz in range(nz) for kx in range(4) if kz or kx]
    around.sort(key=lambda k: -way(k[0], nz) - way(k[1], 4))
    column = [(ky, kc) for ky in range(ny) for kc in range(2) if ky or kc]
    column.sort(key=lambda k: -2 * way(k[0], ny) - k[1])

    def state_at(kz, kx):
        return lax.rem(z + kz, nz) * 4 + lax.rem(x + kx, 4)

    def slab_at(ky, kc):
        return lax.rem(y + ky, ny) * 2 + lax.rem(c + kc, 2)

    barrier = pltpu.get_barrier_semaphore()
    for kz, kx in around:
        for kc in range(2):
            pl.semaphore_signal(barrier, inc=1, device_id=home(state_at(kz, kx), slab_at(0, kc)),
                                device_id_type=MESH)
    for ky, kc in column:
        pl.semaphore_signal(barrier, inc=1, device_id=home(sid, slab_at(ky, kc)),
                            device_id_type=MESH)
    greeted = 2 * len(around) + len(column)

    def part(j, side):
        if j < STRIPS:
            return pl.ds(edge * side, HALO), pl.ds(j * strip, strip)
        if j == STRIPS:
            return pl.ds(HALO + (edge - 2 * HALO) * side, HALO), pl.ds(0, gy)
        return pl.ds(2 * HALO * (1 - side), planes - 2 * HALO), pl.ds(0, gy)

    def part_v(j, side):
        if j == 0:
            return pl.ds(edge * side, HALO)
        return pl.ds(HALO * (1 - side), edge)

    def shifted(rows):
        return pl.ds(HALO + rows.start, rows.size)

    def local_x(j):
        at, rows = part(j, c)
        return pltpu.make_async_copy(x_in.at[0, at, rows], field.at[0, shifted(at), rows],
                                     r_x.at[j])

    def local_v(j):
        at = part_v(j, c)
        return pltpu.make_async_copy(v_in.at[at], pot.at[at], r_v.at[j])

    @pl.when(same)
    def _():
        for j in range(STRIPS + 2):
            local_x(j).start()
        for j in range(2):
            local_v(j).start()

    pl.semaphore_wait(barrier, greeted)

    def swap(j):
        at, rows = part(j, xl)
        return pltpu.make_async_remote_copy(
            src_ref=x_in.at[0, at, rows], dst_ref=field.at[0, shifted(at), rows],
            send_sem=s_x.at[j], recv_sem=r_x.at[j], device_id=(sid, e), device_id_type=MESH)

    def give_v(j):
        at = part_v(j, c)
        return pltpu.make_async_remote_copy(
            src_ref=v_in.at[at], dst_ref=pot.at[at], send_sem=s_v.at[j], recv_sem=r_v.at[j],
            device_id=(b + 2 - 4 * xh, d + 1 - 2 * xl), device_id_type=MESH)

    @pl.when(apart)
    def _():
        for j in range(STRIPS + 2):
            swap(j).start()

    @pl.when(same)
    def _():
        for j in range(2):
            give_v(j).start()

    high, low = circulant(gz)
    wz[0:gz, 0:gz] = high
    wz[gz:, 0:gz] = high
    wz[0:gz, gz:] = low
    wz[gz:, gz:] = jnp.zeros_like(low)
    high, low = circulant(gy)
    wy[0:gy, 0:gy] = high
    wy[0:gy, gy:] = high
    wy[gy:, 0:gy] = low
    wy[gy:, gy:] = jnp.zeros_like(low)

    def send_outer(k, j):
        rows = pl.ds(j * strip, strip)
        return pltpu.make_async_remote_copy(
            src_ref=field.at[k, pl.ds(HALO + edge * c, HALO), rows],
            dst_ref=field.at[k, pl.ds((HALO + planes) * (1 - c), HALO), rows],
            send_sem=s_o.at[k, j], recv_sem=r_o.at[k, j],
            device_id=home(sid, e_out), device_id_type=MESH)

    def send_inner(k):
        return pltpu.make_async_remote_copy(
            src_ref=field.at[k, pl.ds(HALO + edge * (1 - c), HALO)],
            dst_ref=field.at[k, pl.ds((HALO + planes) * c, HALO)],
            send_sem=s_i.at[k], recv_sem=r_i.at[k],
            device_id=home(sid, e_in), device_id_type=MESH)

    def own(rank):
        return rank + c * (planes - 1 - 2 * rank)

    def turned(k, rank, n, terms):
        high, low = [], []
        for t in range(n):
            h, l = halves(field[k - 1, HALO + own(rank + t)])
            high.append(h)
            low.append(l)
        along_z = jnp.dot(
            jnp.concatenate([jnp.concatenate([h, l], 1) for h, l in zip(high, low)], 0),
            wz[...], preferred_element_type=F32)
        along_y = jnp.dot(
            wy[...], jnp.concatenate([jnp.concatenate(high, 1), jnp.concatenate(low, 1)], 0),
            preferred_element_type=F32)
        for t in range(n):
            terms[t] = (along_z[t * gy:(t + 1) * gy, 0:gz] + along_z[t * gy:(t + 1) * gy, gz:]
                        + along_y[0:gy, t * gz:(t + 1) * gz] + along_y[gy:, t * gz:(t + 1) * gz])

    def planes_of(k, rank, n, terms, top=0, bottom=None):
        scale, weight = plan[k - 1]
        shift = -(centre + 1.5 * COEFFS[0]) * scale
        factor = -0.5 * scale
        for r0 in range(top, gy if bottom is None else bottom, 16):
            rows = pl.ds(r0, min(16, strip))
            first = rank - HALO if rank else 0
            near = {j: field[k - 1, HALO + own(j), rows] for j in range(first, rank + n + HALO)}
            for t in range(n):
                here = rank + t
                value = (pot[own(here), rows] * scale + shift) * near[here]
                value = value + factor * terms[t, rows]
                for offset in range(1, HALO + 1):
                    side = near[here + offset]
                    if here - offset in near:
                        side = side + near[here - offset]
                    value = value + (factor * COEFFS[offset]) * side
                if k > 1:
                    value = value - weight * field[k - 2, HALO + own(here), rows]
                field[k, HALO + own(here), rows] = value

    def with_halo(k, j):
        factor = -0.5 * plan[k - 1][0]
        planes_of(k, 0, HALO, t_out, j * strip, (j + 1) * strip)
        send_outer(k - 1, j).wait_recv()
        for r0 in range(0, strip, 16):
            rows = pl.ds(j * strip + r0, min(16, strip))
            near = [field[k - 1, HALO + own(-offset), rows] for offset in range(1, HALO + 1)]
            for rank in range(HALO):
                at = HALO + own(rank)
                value = field[k, at, rows]
                for offset in range(rank + 1, HALO + 1):
                    value = value + (factor * COEFFS[offset]) * near[offset - rank - 1]
                field[k, at, rows] = value
        if k < STEPS:
            send_outer(k, j).start()

    body = planes - 2 * HALO
    t_mid, t_inner = t_in.at[pl.ds(0, body)], t_in.at[pl.ds(body, HALO)]

    def turn_outer(k):
        turned(k, 0, HALO, t_out)

    def turn_inner(k):
        turned(k, HALO, body, t_mid)
        turned(k, edge, HALO, t_inner)

    first, second, whole = pl.ds(0, half), pl.ds(half, half), pl.ds(0, gy)

    def spread(to, rows, j):
        return pltpu.make_async_remote_copy(
            src_ref=field.at[STEPS, HALO + to, rows], dst_ref=recv.at[sid, rows],
            send_sem=s_f.at[to, j], recv_sem=r_f.at[sid, j],
            device_id=home(to, e), device_id_type=MESH)

    def spread_ranks(rank, n, rows, j, act):
        for k in range(n):
            to = own(rank + lax.rem(k + z + x, n))

            @pl.when(to != sid)
            def _():
                act(spread(to, rows, j))

    def start(copy):
        copy.start()

    def wait_send(copy):
        copy.wait_send()

    for j in range(STRIPS):
        local_x(j).wait()
        send_outer(0, j).start()
    turn_outer(1)
    local_v(0).wait()
    local_x(STRIPS).wait()
    for j in range(STRIPS):
        with_halo(1, j)
    local_x(STRIPS + 1).wait()
    send_inner(0).start()
    turn_inner(1)
    local_v(1).wait()
    planes_of(1, HALO, body, t_mid)
    send_inner(0).wait_recv()
    planes_of(1, edge, HALO, t_inner)
    send_inner(1).start()

    for k in range(2, STEPS):
        turn_outer(k)
        with_halo(k, 0)
        turn_inner(k)
        planes_of(k, HALO, body, t_mid)
        with_halo(k, 1)
        send_inner(k - 1).wait_recv()
        planes_of(k, edge, HALO, t_inner)
        send_inner(k).start()
        for j in range(2, STRIPS - 1):
            with_halo(k, j)
        if k < STEPS - 1:
            with_halo(k, STRIPS - 1)
    turn_inner(STEPS)

    deep = HALO - EARLY
    send_inner(STEPS - 1).wait_recv()
    planes_of(STEPS, planes - EARLY, EARLY, t_inner.at[pl.ds(deep, EARLY)])
    spread_ranks(planes - EARLY, EARLY, whole, 0, start)
    with_halo(STEPS - 1, STRIPS - 1)
    planes_of(STEPS, HALO, body + deep, t_in.at[pl.ds(0, body + deep)])
    spread_ranks(HALO, body + deep, whole, 0, start)
    turn_outer(STEPS)
    for j in range(STRIPS // 2):
        with_halo(STEPS, j)
    spread_ranks(0, HALO, first, 0, start)
    for j in range(STRIPS // 2, STRIPS):
        with_halo(STEPS, j)
    spread_ranks(0, HALO, second, 1, start)
    recv[pl.ds(sid, 1)] = field[STEPS, pl.ds(HALO + sid, 1)]

    tall = nb * 8
    wide = half // 8 * gz
    late = jnp.where(c == 0, sid < HALO, sid >= edge)

    def arrived(rows, j):
        for kz, kx in around:
            at = recv.at[state_at(kz, kx), rows]
            pltpu.make_async_copy(at, at, r_f.at[state_at(kz, kx), j]).wait()

    def products(j):
        high, low = [], []
        for g in range(half // 8):
            h, l = halves(recv[:, j * half + 8 * g:j * half + 8 * g + 8, :].reshape(tall, gz))
            high.append(h)
            low.append(l)
        both = jnp.concatenate([jnp.concatenate(high, 1), jnp.concatenate(low, 1)], 0)
        split[:, j * wide:(j + 1) * wide] = both
        return lax.dot_general(both, both, (((1,), (1,)), ((), ())), preferred_element_type=F32)

    @pl.when(late)
    def _():
        arrived(first, 0)

    @pl.when(jnp.logical_not(late))
    def _():
        arrived(whole, 0)

    total = products(0)

    @pl.when(late)
    def _():
        arrived(second, 1)

    total = total + products(1)
    total = total[0:tall, 0:tall] + total[0:tall, tall:] + total[tall:, 0:tall] + total[tall:, tall:]
    at_row = lax.broadcasted_iota(jnp.int32, (tall, tall), 0)
    at_col = lax.broadcasted_iota(jnp.int32, (tall, tall), 1)
    match = lax.rem(at_row, 8) == lax.rem(at_col, 8)
    gb[pl.ds(e, 1)] = jnp.where(match, total, 0.0).reshape(nb, 8, tall).sum(axis=1)[None]

    def share_b(ky, kc):
        to = slab_at(ky, kc)
        return pltpu.make_async_remote_copy(
            src_ref=gb.at[e], dst_ref=gb.at[e], send_sem=s_b.at[to], recv_sem=r_b.at[e],
            device_id=home(sid, to), device_id_type=MESH)

    for ky, kc in column:
        share_b(ky, kc).start()
    for ky, kc in reversed(column):
        origin = slab_at(ky, kc)
        pltpu.make_async_copy(gb.at[origin], gb.at[origin], r_b.at[origin]).wait()
    ga[pl.ds(sid, 1)] = jnp.sum(gb[...], axis=0, keepdims=True)

    def share_a(kz, kx):
        to = state_at(kz, kx)
        return pltpu.make_async_remote_copy(
            src_ref=ga.at[sid], dst_ref=ga.at[sid], send_sem=s_a.at[to], recv_sem=r_a.at[sid],
            device_id=home(to, e), device_id_type=MESH)

    for kz, kx in around:
        share_a(kz, kx).start()
    same_state = (at_row // 8 == at_col // 8).astype(F32)
    for kz, kx in reversed(around):
        origin = state_at(kz, kx)
        pltpu.make_async_copy(ga.at[origin], ga.at[origin], r_a.at[origin]).wait()

    whole_sum = jnp.sum(ga[...], axis=0) / float(planes * nd * gy * gz)
    matrix = jnp.dot(whole_sum, same_state, precision=lax.Precision.HIGHEST,
                     preferred_element_type=F32)

    sub = lax.broadcasted_iota(jnp.int32, (nb, tall), 0)
    lane = lax.broadcasted_iota(jnp.int32, (nb, tall), 1)
    work = matrix
    inverse = (sub == lane // 8).astype(F32)
    for k in range(nb - 1):
        factor = work[:, 8 * k:8 * k + 1] / work[k:k + 1, 8 * k:8 * k + 1]
        factor = jnp.where(sub > k, factor, 0.0)
        work = work - factor * work[k:k + 1, :]
        inverse = inverse - factor * inverse[k:k + 1, :]
    diagonal = jnp.sum(jnp.where(lane == 8 * sub, work, 0.0), axis=1, keepdims=True)
    inverse = inverse / jnp.sqrt(diagonal)

    inverse = jnp.broadcast_to(inverse[:, None, :], (nb, 8, tall)).reshape(tall, tall)
    high, low = halves(jnp.where(match, inverse, 0.0))
    left = jnp.concatenate([jnp.concatenate([high, high], 1),
                            jnp.concatenate([low, jnp.zeros_like(low)], 1)], 0)

    back = [(kz, h, t) for kz in range(nz) for h in range(2) for t in range(2)]
    back.sort(key=lambda k: (-way(k[0], nz) - k[1], -k[2]))

    def give_back(kz, h, t, j):
        state = lax.rem(z + kz, nz) * 4 + lax.rem(xh + h, 2) * 2 + lax.rem(c + t, 2)
        rows = (first, second)[j]
        return pltpu.make_async_remote_copy(
            src_ref=ortho.at[state, rows], dst_ref=out.at[0, sid, rows],
            send_sem=s_r.at[state, j], recv_sem=r_r.at[sid, j], device_id=(state, e),
            device_id_type=MESH)

    def own_back(j):
        rows = (first, second)[j]
        return pltpu.make_async_copy(ortho.at[b, rows], out.at[0, b, rows], r_r.at[b, j])

    for j in range(2):
        value = jnp.dot(left, split[:, j * wide:(j + 1) * wide], preferred_element_type=F32)
        for g in range(half // 8):
            at = slice(g * gz, (g + 1) * gz)
            ortho[:, j * half + 8 * g:j * half + 8 * g + 8, :] = (
                value[0:tall, at] + value[tall:, at]).reshape(nb, 8, gz)
        for item in back[:-1]:
            give_back(*item, j).start()

        @pl.when(same)
        def _():
            own_back(j).start()

        @pl.when(apart)
        def _():
            give_back(*back[-1], j).start()

    pick_row = lax.broadcasted_iota(jnp.int32, (tall, nb), 0)
    pick_col = lax.broadcasted_iota(jnp.int32, (tall, nb), 1)
    corr[...] = jnp.dot(matrix, (pick_row == 8 * pick_col).astype(F32),
                        precision=lax.Precision.HIGHEST, preferred_element_type=F32)

    @pl.when(apart)
    def _():
        for j in range(STRIPS + 2):
            swap(j).wait_send()

    @pl.when(same)
    def _():
        for j in range(2):
            give_v(j).wait_send()

    for k in range(STEPS):
        for j in range(STRIPS):
            send_outer(k, j).wait_send()
        send_inner(k).wait_send()
    spread_ranks(HALO, edge, whole, 0, wait_send)
    spread_ranks(0, HALO, first, 0, wait_send)
    spread_ranks(0, HALO, second, 1, wait_send)
    for ky, kc in column:
        share_b(ky, kc).wait_send()
    for kz, kx in around:
        share_a(kz, kx).wait_send()

    for j in range(2):
        for item in back[:-1]:
            give_back(*item, j).wait_send()

        @pl.when(apart)
        def _():
            give_back(*back[-1], j).wait_send()

        @pl.loop(0, nb)
        def _(p):
            at = out.at[0, p, (first, second)[j]]
            pltpu.make_async_copy(at, at, r_r.at[p, j]).wait()


def shards(orbitals, potential):
    nb, nd = lax.axis_size("band"), lax.axis_size("dom")
    planes, gy, gz = potential.shape
    tall = nb * 8
    dma = pltpu.SemaphoreType.DMA
    any_space = pl.BlockSpec(memory_space=pl.ANY)
    hbm = pl.BlockSpec(memory_space=pltpu.HBM)
    return pl.pallas_call(
        lambda *refs: kernel(nb, nd, *refs),
        out_shape=(jax.ShapeDtypeStruct(orbitals.shape, F32),
                   jax.ShapeDtypeStruct((nb, nb), F32)),
        in_specs=[hbm, hbm],
        out_specs=(any_space, pl.BlockSpec(memory_space=pltpu.VMEM)),
        scratch_shapes=[
            pltpu.VMEM((STEPS + 1, planes + 2 * HALO, gy, gz), F32),
            pltpu.VMEM((planes, gy, gz), F32),
            pltpu.VMEM((2 * gz, 2 * gz), BF16),
            pltpu.VMEM((2 * gy, 2 * gy), BF16),
            pltpu.VMEM((HALO, gy, gz), F32),
            pltpu.VMEM((planes - HALO, gy, gz), F32),
            pltpu.VMEM((nb, gy, gz), F32),
            pltpu.VMEM((2 * tall, gy // 8 * gz), BF16),
            pltpu.VMEM((nb, gy, gz), F32),
            pltpu.VMEM((nb, nb, tall), F32),
            pltpu.VMEM((nd, nb, tall), F32),
            dma((STRIPS + 2,)), dma((STRIPS + 2,)),
            dma((2,)), dma((2,)),
            dma((STEPS, STRIPS)), dma((STEPS, STRIPS)),
            dma((STEPS,)), dma((STEPS,)),
            dma((nb, 2)), dma((nb, 2)),
            dma((nb,)), dma((nb,)),
            dma((nd,)), dma((nd,)),
            dma((nb, 2)), dma((nb, 2)),
        ],
        compiler_params=pltpu.CompilerParams(
            collective_id=0, has_side_effects=True, vmem_limit_bytes=52 * 1024 * 1024),
        cost_estimate=pl.CostEstimate(flops=2 * 10**9, bytes_accessed=4 * 10**6,
                                      transcendentals=0),
    )(orbitals, potential)


def solution(mesh):
    placed = (P("band", "dom", None, None), P("dom", None, None))
    return jax.shard_map(
        shards,
        mesh=mesh,
        in_specs=placed,
        out_specs=(P("band", "dom", None, None), P()),
        check_vma=False,
    )
```

```python
import jax
import jax.numpy as jnp
from jax import lax
from jax.experimental import pallas as pl
from jax.experimental.pallas import tpu as pltpu
from jax.sharding import PartitionSpec as P

STEPS = 4
COEFFS = (
    -5369.0 / 1800.0,
    12.0 / 7.0,
    -15.0 / 56.0,
    10.0 / 189.0,
    -1.0 / 112.0,
    2.0 / 1925.0,
    -1.0 / 16632.0,
)
LOWER_EDGE = -3.5
CUT_EDGE = 0.5
UPPER_EDGE = 11.0
HALO = 6
STRIPS = 4
EARLY = 4
MESH = pl.DeviceIdType.MESH
F32 = jnp.float32
BF16 = jnp.bfloat16


def recurrence(count):
    half_width = (UPPER_EDGE - CUT_EDGE) / 2.0
    centre = (UPPER_EDGE + CUT_EDGE) / 2.0
    sigma_now = half_width / (LOWER_EDGE - centre)
    gamma_value = 2.0 / sigma_now
    plan = [(sigma_now / half_width, 0.0)]
    for number in range(count - 1):
        sigma_next = 1.0 / (gamma_value - sigma_now)
        plan.append((2.0 * sigma_next / half_width, sigma_now * sigma_next))
        sigma_now = sigma_next
    return (centre, plan)


def halves(value):
    high = value.astype(BF16)
    return high, (value - high.astype(F32)).astype(BF16)


def circulant(size):
    row = lax.broadcasted_iota(jnp.int32, (size, size), 0)
    col = lax.broadcasted_iota(jnp.int32, (size, size), 1)
    gap = jnp.abs(row - col)
    gap = jnp.minimum(gap, size - gap)
    value = jnp.zeros((size, size), F32)
    for offset in range(1, HALO + 1):
        value = jnp.where(gap == offset, COEFFS[offset], value)
    return halves(value)


def kernel(nb, nd, x_in, v_in, out, corr, field, pot, wz, wy, t_out, t_in, recv, split, ortho,
           ga, gb, s_x, r_x, s_v, r_v, s_o, r_o, s_i, r_i, s_f, r_f, s_a, r_a, s_b, r_b,
           s_r, r_r, told):
    planes, gy, gz = v_in.shape
    edge = planes - HALO
    nz, ny = nb // 4, nd // 2
    strip = gy // STRIPS
    half = gy // 2
    centre, plan = recurrence(STEPS)
    b, d = lax.axis_index("band"), lax.axis_index("dom")
    c, xl = lax.rem(b, 2), lax.rem(d, 2)
    xh = lax.rem(b // 2, 2)
    y, z = d // 2, b // 4
    x = 2 * xh + xl
    sid = b - c + xl
    e = d - xl + c
    same = c == xl
    apart = jnp.logical_not(same)

    def home(state, slab):
        sp, ep = lax.rem(state, 2), lax.rem(slab, 2)
        return (state - sp + ep, slab - ep + sp)

    e_out = lax.rem(e + 2 * c - 1 + nd, nd)
    e_in = e + 1 - 2 * c

    def way(k, n):
        return min(k, n - k)

    around = [(kz, kx) for kz in range(nz) for kx in range(4) if kz or kx]
    around.sort(key=lambda k: -way(k[0], nz) - way(k[1], 4))
    column = [(ky, kc) for ky in range(ny) for kc in range(2) if ky or kc]
    column.sort(key=lambda k: -2 * way(k[0], ny) - k[1])

    def state_at(kz, kx):
        return lax.rem(z + kz, nz) * 4 + lax.rem(x + kx, 4)

    def slab_at(ky, kc):
        return lax.rem(y + ky, ny) * 2 + lax.rem(c + kc, 2)

    def chip(kz, kx):
        return home(state_at(kz, kx), e)

    barrier = pltpu.get_barrier_semaphore()

    @pl.when(apart)
    def _():
        pl.semaphore_signal(barrier, inc=1, device_id=(sid, e), device_id_type=MESH)

    beside_z = [chip(1, 0), chip(nz - 1, 0)]
    beside_x = [chip(0, 1), chip(0, 3)]
    beside_c = [home(sid, e_in)]
    for who in beside_x + beside_z + beside_c + [home(sid, e_out)]:
        pl.semaphore_signal(barrier, inc=1, device_id=who, device_id_type=MESH)
    greeted = jnp.where(same, 6, 7)

    rounds = [beside_z, beside_x, beside_x, beside_c]

    def tell(i):
        for who in rounds[i]:
            pl.semaphore_signal(told.at[i], inc=1, device_id=who, device_id_type=MESH)

    def hear(i):
        pl.semaphore_wait(told.at[i], len(rounds[i]))

    def part(j, side):
        if j < STRIPS:
            return pl.ds(edge * side, HALO), pl.ds(j * strip, strip)
        if j == STRIPS:
            return pl.ds(HALO + (edge - 2 * HALO) * side, HALO), pl.ds(0, gy)
        return pl.ds(2 * HALO * (1 - side), planes - 2 * HALO), pl.ds(0, gy)

    def part_v(j, side):
        if j == 0:
            return pl.ds(edge * side, HALO)
        return pl.ds(HALO * (1 - side), edge)

    def shifted(rows):
        return pl.ds(HALO + rows.start, rows.size)

    def local_x(j):
        at, rows = part(j, c)
        return pltpu.make_async_copy(x_in.at[0, at, rows], field.at[0, shifted(at), rows],
                                     r_x.at[j])

    def local_v(j):
        at = part_v(j, c)
        return pltpu.make_async_copy(v_in.at[at], pot.at[at], r_v.at[j])

    @pl.when(same)
    def _():
        for j in range(STRIPS + 2):
            local_x(j).start()
        for j in range(2):
            local_v(j).start()

    pl.semaphore_wait(barrier, greeted)

    def swap(j):
        at, rows = part(j, xl)
        return pltpu.make_async_remote_copy(
            src_ref=x_in.at[0, at, rows], dst_ref=field.at[0, shifted(at), rows],
            send_sem=s_x.at[j], recv_sem=r_x.at[j], device_id=(sid, e), device_id_type=MESH)

    def give_v(j):
        at = part_v(j, c)
        return pltpu.make_async_remote_copy(
            src_ref=v_in.at[at], dst_ref=pot.at[at], send_sem=s_v.at[j], recv_sem=r_v.at[j],
            device_id=(b + 2 - 4 * xh, d + 1 - 2 * xl), device_id_type=MESH)

    @pl.when(apart)
    def _():
        for j in range(STRIPS + 2):
            swap(j).start()

    @pl.when(same)
    def _():
        for j in range(2):
            give_v(j).start()

    tell(0)
    high, low = circulant(gz)
    wz[0:gz, 0:gz] = high
    wz[gz:, 0:gz] = high
    wz[0:gz, gz:] = low
    wz[gz:, gz:] = jnp.zeros_like(low)
    high, low = circulant(gy)
    wy[0:gy, 0:gy] = high
    wy[0:gy, gy:] = high
    wy[gy:, 0:gy] = low
    wy[gy:, gy:] = jnp.zeros_like(low)

    def send_outer(k, j):
        rows = pl.ds(j * strip, strip)
        return pltpu.make_async_remote_copy(
            src_ref=field.at[k, pl.ds(HALO + edge * c, HALO), rows],
            dst_ref=field.at[k, pl.ds((HALO + planes) * (1 - c), HALO), rows],
            send_sem=s_o.at[k, j], recv_sem=r_o.at[k, j],
            device_id=home(sid, e_out), device_id_type=MESH)

    def send_inner(k):
        return pltpu.make_async_remote_copy(
            src_ref=field.at[k, pl.ds(HALO + edge * (1 - c), HALO)],
            dst_ref=field.at[k, pl.ds((HALO + planes) * c, HALO)],
            send_sem=s_i.at[k], recv_sem=r_i.at[k],
            device_id=home(sid, e_in), device_id_type=MESH)

    def own(rank):
        return rank + c * (planes - 1 - 2 * rank)

    def turned(k, rank, n, terms):
        high, low = [], []
        for t in range(n):
            h, l = halves(field[k - 1, HALO + own(rank + t)])
            high.append(h)
            low.append(l)
        along_z = jnp.dot(
            jnp.concatenate([jnp.concatenate([h, l], 1) for h, l in zip(high, low)], 0),
            wz[...], preferred_element_type=F32)
        along_y = jnp.dot(
            wy[...], jnp.concatenate([jnp.concatenate(high, 1), jnp.concatenate(low, 1)], 0),
            preferred_element_type=F32)
        for t in range(n):
            terms[t] = (along_z[t * gy:(t + 1) * gy, 0:gz] + along_z[t * gy:(t + 1) * gy, gz:]
                        + along_y[0:gy, t * gz:(t + 1) * gz] + along_y[gy:, t * gz:(t + 1) * gz])

    def planes_of(k, rank, n, terms, top=0, bottom=None):
        scale, weight = plan[k - 1]
        shift = -(centre + 1.5 * COEFFS[0]) * scale
        factor = -0.5 * scale
        for r0 in range(top, gy if bottom is None else bottom, 16):
            rows = pl.ds(r0, min(16, strip))
            first = rank - HALO if rank else 0
            near = {j: field[k - 1, HALO + own(j), rows] for j in range(first, rank + n + HALO)}
            for t in range(n):
                here = rank + t
                value = (pot[own(here), rows] * scale + shift) * near[here]
                value = value + factor * terms[t, rows]
                for offset in range(1, HALO + 1):
                    side = near[here + offset]
                    if here - offset in near:
                        side = side + near[here - offset]
                    value = value + (factor * COEFFS[offset]) * side
                if k > 1:
                    value = value - weight * field[k - 2, HALO + own(here), rows]
                field[k, HALO + own(here), rows] = value

    def with_halo(k, j):
        factor = -0.5 * plan[k - 1][0]
        planes_of(k, 0, HALO, t_out, j * strip, (j + 1) * strip)
        send_outer(k - 1, j).wait_recv()
        for r0 in range(0, strip, 16):
            rows = pl.ds(j * strip + r0, min(16, strip))
            near = [field[k - 1, HALO + own(-offset), rows] for offset in range(1, HALO + 1)]
            for rank in range(HALO):
                at = HALO + own(rank)
                value = field[k, at, rows]
                for offset in range(rank + 1, HALO + 1):
                    value = value + (factor * COEFFS[offset]) * near[offset - rank - 1]
                field[k, at, rows] = value
        if k < STEPS:
            send_outer(k, j).start()

    body = planes - 2 * HALO
    t_mid, t_inner = t_in.at[pl.ds(0, body)], t_in.at[pl.ds(body, HALO)]

    def turn_outer(k):
        turned(k, 0, HALO, t_out)

    def turn_inner(k):
        turned(k, HALO, body, t_mid)
        turned(k, edge, HALO, t_inner)

    first, second, whole = pl.ds(0, half), pl.ds(half, half), pl.ds(0, gy)

    def dealt(rank):
        return lax.rem(rank, 4) * 4 + lax.rem(lax.rem(rank, 4) + rank // 4 + 2 * c, 4)

    my_rank = 4 * lax.rem(x - z + 8 - 2 * c, 4) + z
    my_plane = own(my_rank)

    def spread(rank, rows, j):
        to = dealt(rank)
        return pltpu.make_async_remote_copy(
            src_ref=field.at[STEPS, HALO + own(rank), rows], dst_ref=recv.at[sid, rows],
            send_sem=s_f.at[to, j], recv_sem=r_f.at[sid, j],
            device_id=home(to, e), device_id_type=MESH)

    def spread_ranks(rank, n, rows, j, act):
        for k in range(n):
            at = rank + lax.rem(k + z + x, n)

            @pl.when(at != my_rank)
            def _():
                act(spread(at, rows, j))

    def start(copy):
        copy.start()

    def wait_send(copy):
        copy.wait_send()

    for j in range(STRIPS):
        local_x(j).wait()
        send_outer(0, j).start()
    turn_outer(1)
    local_v(0).wait()
    local_x(STRIPS).wait()
    for j in range(STRIPS):
        with_halo(1, j)
    hear(0)
    tell(1)
    local_x(STRIPS + 1).wait()
    send_inner(0).start()
    turn_inner(1)
    local_v(1).wait()
    planes_of(1, HALO, body, t_mid)
    send_inner(0).wait_recv()
    planes_of(1, edge, HALO, t_inner)
    send_inner(1).start()

    for k in range(2, STEPS):
        last = k == STEPS - 1
        turn_outer(k)
        with_halo(k, 0)
        hear(k - 1)
        tell(k)
        if k == 2:
            turn_inner(k)
        planes_of(k, HALO, body, t_mid)
        if not last:
            with_halo(k, 1)
        send_inner(k - 1).wait_recv()
        planes_of(k, edge, HALO, t_inner)
        send_inner(k).start()
        if last:
            with_halo(k, 1)
            turn_inner(k + 1)
        for j in range(2, STRIPS - 1):
            with_halo(k, j)
        if not last:
            turn_inner(k + 1)
            with_halo(k, STRIPS - 1)

    hear(3)

    deep = HALO - EARLY
    send_inner(STEPS - 1).wait_recv()
    planes_of(STEPS, planes - EARLY, EARLY, t_inner.at[pl.ds(deep, EARLY)])
    spread_ranks(planes - EARLY, EARLY, whole, 0, start)
    with_halo(STEPS - 1, STRIPS - 1)
    planes_of(STEPS, HALO, body + deep, t_in.at[pl.ds(0, body + deep)])
    spread_ranks(HALO, body + deep, whole, 0, start)
    turn_outer(STEPS)
    for j in range(STRIPS // 2):
        with_halo(STEPS, j)
    spread_ranks(0, HALO, first, 0, start)
    for j in range(STRIPS // 2, STRIPS):
        with_halo(STEPS, j)
    spread_ranks(0, HALO, second, 1, start)
    recv[pl.ds(sid, 1)] = field[STEPS, pl.ds(HALO + my_plane, 1)]

    tall = nb * 8
    wide = half // 8 * gz
    late = my_rank < HALO

    def arrived(rows, j):
        for kz, kx in around:
            at = recv.at[state_at(kz, kx), rows]
            pltpu.make_async_copy(at, at, r_f.at[state_at(kz, kx), j]).wait()

    def products(j):
        high, low = [], []
        for g in range(half // 8):
            h, l = halves(recv[:, j * half + 8 * g:j * half + 8 * g + 8, :].reshape(tall, gz))
            high.append(h)
            low.append(l)
        both = jnp.concatenate([jnp.concatenate(high, 1), jnp.concatenate(low, 1)], 0)
        split[:, j * wide:(j + 1) * wide] = both
        return lax.dot_general(both, both, (((1,), (1,)), ((), ())), preferred_element_type=F32)

    @pl.when(late)
    def _():
        arrived(first, 0)

    @pl.when(jnp.logical_not(late))
    def _():
        arrived(whole, 0)

    total = products(0)

    @pl.when(late)
    def _():
        arrived(second, 1)

    total = total + products(1)
    total = total[0:tall, 0:tall] + total[0:tall, tall:] + total[tall:, 0:tall] + total[tall:, tall:]
    at_row = lax.broadcasted_iota(jnp.int32, (tall, tall), 0)
    at_col = lax.broadcasted_iota(jnp.int32, (tall, tall), 1)
    match = lax.rem(at_row, 8) == lax.rem(at_col, 8)
    total = jnp.where(match, total, 0.0).reshape(nb, 8, tall).sum(axis=1)
    total = total + pltpu.roll(total, tall - 4, 1)
    lower = lax.rem(lax.broadcasted_iota(jnp.int32, (nb // 2, tall), 1), 8) < 4
    gb[pl.ds(e, 1)] = jnp.where(
        lower, total[0:nb // 2], pltpu.roll(total[nb // 2:], 4, 1))[None]

    def share_b(ky, kc):
        to = slab_at(ky, kc)
        return pltpu.make_async_remote_copy(
            src_ref=gb.at[e], dst_ref=gb.at[e], send_sem=s_b.at[to], recv_sem=r_b.at[e],
            device_id=home(sid, to), device_id_type=MESH)

    for ky, kc in column:
        share_b(ky, kc).start()
    for ky, kc in reversed(column):
        origin = slab_at(ky, kc)
        pltpu.make_async_copy(gb.at[origin], gb.at[origin], r_b.at[origin]).wait()
    ga[pl.ds(sid, 1)] = jnp.sum(gb[...], axis=0, keepdims=True)

    def share_a(kz, kx):
        to = state_at(kz, kx)
        return pltpu.make_async_remote_copy(
            src_ref=ga.at[sid], dst_ref=ga.at[sid], send_sem=s_a.at[to], recv_sem=r_a.at[sid],
            device_id=home(to, e), device_id_type=MESH)

    for kz, kx in around:
        share_a(kz, kx).start()
    same_state = (at_row // 8 == at_col // 8).astype(F32)
    for kz, kx in reversed(around):
        origin = state_at(kz, kx)
        pltpu.make_async_copy(ga.at[origin], ga.at[origin], r_a.at[origin]).wait()

    whole_sum = jnp.sum(ga[...], axis=0) / float(planes * nd * gy * gz)
    whole_sum = jnp.concatenate(
        [jnp.where(lower, whole_sum, 0.0), jnp.where(lower, 0.0, whole_sum)], 0)
    matrix = jnp.dot(whole_sum, same_state, precision=lax.Precision.HIGHEST,
                     preferred_element_type=F32)

    sub = lax.broadcasted_iota(jnp.int32, (nb, tall), 0)
    lane = lax.broadcasted_iota(jnp.int32, (nb, tall), 1)
    work = matrix
    inverse = (sub == lane // 8).astype(F32)
    for k in range(nb - 1):
        factor = work[:, 8 * k:8 * k + 1] / work[k:k + 1, 8 * k:8 * k + 1]
        factor = jnp.where(sub > k, factor, 0.0)
        work = work - factor * work[k:k + 1, :]
        inverse = inverse - factor * inverse[k:k + 1, :]
    diagonal = jnp.sum(jnp.where(lane == 8 * sub, work, 0.0), axis=1, keepdims=True)
    inverse = inverse / jnp.sqrt(diagonal)

    inverse = jnp.broadcast_to(inverse[:, None, :], (nb, 8, tall)).reshape(tall, tall)
    high, low = halves(jnp.where(match, inverse, 0.0))
    left = jnp.concatenate([jnp.concatenate([high, high], 1),
                            jnp.concatenate([low, jnp.zeros_like(low)], 1)], 0)

    back = [(kz, h, t) for kz in range(nz) for h in range(2) for t in range(2)]
    back.sort(key=lambda k: (-way(k[0], nz) - k[1], -k[2]))

    def give_back(kz, h, t, j):
        state = lax.rem(z + kz, nz) * 4 + lax.rem(xh + h, 2) * 2 + lax.rem(c + t, 2)
        rows = (first, second)[j]
        return pltpu.make_async_remote_copy(
            src_ref=ortho.at[state, rows], dst_ref=out.at[0, my_plane, rows],
            send_sem=s_r.at[state, j], recv_sem=r_r.at[my_plane, j], device_id=(state, e),
            device_id_type=MESH)

    def own_back(j):
        rows = (first, second)[j]
        return pltpu.make_async_copy(
            ortho.at[b, rows], out.at[0, my_plane, rows], r_r.at[my_plane, j])

    for j in range(2):
        value = jnp.dot(left, split[:, j * wide:(j + 1) * wide], preferred_element_type=F32)
        for g in range(half // 8):
            at = slice(g * gz, (g + 1) * gz)
            ortho[:, j * half + 8 * g:j * half + 8 * g + 8, :] = (
                value[0:tall, at] + value[tall:, at]).reshape(nb, 8, gz)
        for item in back[:-1]:
            give_back(*item, j).start()

        @pl.when(same)
        def _():
            own_back(j).start()

        @pl.when(apart)
        def _():
            give_back(*back[-1], j).start()

    pick_row = lax.broadcasted_iota(jnp.int32, (tall, nb), 0)
    pick_col = lax.broadcasted_iota(jnp.int32, (tall, nb), 1)
    corr[...] = jnp.dot(matrix, (pick_row == 8 * pick_col).astype(F32),
                        precision=lax.Precision.HIGHEST, preferred_element_type=F32)

    @pl.when(apart)
    def _():
        for j in range(STRIPS + 2):
            swap(j).wait_send()

    @pl.when(same)
    def _():
        for j in range(2):
            give_v(j).wait_send()

    for k in range(STEPS):
        for j in range(STRIPS):
            send_outer(k, j).wait_send()
        send_inner(k).wait_send()
    spread_ranks(HALO, edge, whole, 0, wait_send)
    spread_ranks(0, HALO, first, 0, wait_send)
    spread_ranks(0, HALO, second, 1, wait_send)
    for ky, kc in column:
        share_b(ky, kc).wait_send()
    for kz, kx in around:
        share_a(kz, kx).wait_send()

    for j in range(2):
        for item in back[:-1]:
            give_back(*item, j).wait_send()

        @pl.when(apart)
        def _():
            give_back(*back[-1], j).wait_send()

        @pl.loop(0, nb)
        def _(p):
            at = out.at[0, p, (first, second)[j]]
            pltpu.make_async_copy(at, at, r_r.at[p, j]).wait()


def shards(orbitals, potential):
    nb, nd = lax.axis_size("band"), lax.axis_size("dom")
    planes, gy, gz = potential.shape
    tall = nb * 8
    dma = pltpu.SemaphoreType.DMA
    any_space = pl.BlockSpec(memory_space=pl.ANY)
    hbm = pl.BlockSpec(memory_space=pltpu.HBM)
    return pl.pallas_call(
        lambda *refs: kernel(nb, nd, *refs),
        out_shape=(jax.ShapeDtypeStruct(orbitals.shape, F32),
                   jax.ShapeDtypeStruct((nb, nb), F32)),
        in_specs=[hbm, hbm],
        out_specs=(any_space, pl.BlockSpec(memory_space=pltpu.VMEM)),
        scratch_shapes=[
            pltpu.VMEM((STEPS + 1, planes + 2 * HALO, gy, gz), F32),
            pltpu.VMEM((planes, gy, gz), F32),
            pltpu.VMEM((2 * gz, 2 * gz), BF16),
            pltpu.VMEM((2 * gy, 2 * gy), BF16),
            pltpu.VMEM((HALO, gy, gz), F32),
            pltpu.VMEM((planes - HALO, gy, gz), F32),
            pltpu.VMEM((nb, gy, gz), F32),
            pltpu.VMEM((2 * tall, gy // 8 * gz), BF16),
            pltpu.VMEM((nb, gy, gz), F32),
            pltpu.VMEM((nb, nb // 2, tall), F32),
            pltpu.VMEM((nd, nb // 2, tall), F32),
            dma((STRIPS + 2,)), dma((STRIPS + 2,)),
            dma((2,)), dma((2,)),
            dma((STEPS, STRIPS)), dma((STEPS, STRIPS)),
            dma((STEPS,)), dma((STEPS,)),
            dma((nb, 2)), dma((nb, 2)),
            dma((nb,)), dma((nb,)),
            dma((nd,)), dma((nd,)),
            dma((nb, 2)), dma((nb, 2)),
            pltpu.SemaphoreType.REGULAR((4,)),
        ],
        compiler_params=pltpu.CompilerParams(
            collective_id=0, has_side_effects=True, vmem_limit_bytes=52 * 1024 * 1024),
        cost_estimate=pl.CostEstimate(flops=2 * 10**9, bytes_accessed=4 * 10**6,
                                      transcendentals=0),
    )(orbitals, potential)


def solution(mesh):
    placed = (P("band", "dom", None, None), P("dom", None, None))
    return jax.shard_map(
        shards,
        mesh=mesh,
        in_specs=placed,
        out_specs=(P("band", "dom", None, None), P()),
        check_vma=False,
    )
```

```python
import jax
import jax.numpy as jnp
from jax import lax
from jax.experimental import pallas as pl
from jax.experimental.pallas import tpu as pltpu
from jax.sharding import PartitionSpec as P

STEPS = 4
COEFFS = (
    -5369.0 / 1800.0,
    12.0 / 7.0,
    -15.0 / 56.0,
    10.0 / 189.0,
    -1.0 / 112.0,
    2.0 / 1925.0,
    -1.0 / 16632.0,
)
LOWER_EDGE = -3.5
CUT_EDGE = 0.5
UPPER_EDGE = 11.0
HALO = 6
STRIPS = 4
EARLY = 4
PIECES = 2
MESH = pl.DeviceIdType.MESH
F32 = jnp.float32
BF16 = jnp.bfloat16


def recurrence(count):
    half_width = (UPPER_EDGE - CUT_EDGE) / 2.0
    centre = (UPPER_EDGE + CUT_EDGE) / 2.0
    sigma_now = half_width / (LOWER_EDGE - centre)
    gamma_value = 2.0 / sigma_now
    plan = [(sigma_now / half_width, 0.0)]
    for number in range(count - 1):
        sigma_next = 1.0 / (gamma_value - sigma_now)
        plan.append((2.0 * sigma_next / half_width, sigma_now * sigma_next))
        sigma_now = sigma_next
    return (centre, plan)


def halves(value):
    high = value.astype(BF16)
    return high, (value - high.astype(F32)).astype(BF16)


def circulant(size):
    row = lax.broadcasted_iota(jnp.int32, (size, size), 0)
    col = lax.broadcasted_iota(jnp.int32, (size, size), 1)
    gap = jnp.abs(row - col)
    gap = jnp.minimum(gap, size - gap)
    value = jnp.zeros((size, size), F32)
    for offset in range(1, HALO + 1):
        value = jnp.where(gap == offset, COEFFS[offset], value)
    return halves(value)


def kernel(nb, nd, x_in, v_in, out, corr, field0, field1, field2, field3, field4, pot, wz, wy, t_out, t_in, recv, split, ortho,
           ga, gb, s_x, r_x, s_v, r_v, s_o, r_o, s_i, r_i, s_f, r_f, s_a, r_a, s_b, r_b,
           s_r, r_r, told):
    field = (field0, field1, field2, field3, field4)
    planes, gy, gz = v_in.shape
    edge = planes - HALO
    nz, ny = nb // 4, nd // 2
    strip = gy // STRIPS
    half = gy // 2
    centre, plan = recurrence(STEPS)
    b, d = lax.axis_index("band"), lax.axis_index("dom")
    c, xl = lax.rem(b, 2), lax.rem(d, 2)
    xh = lax.rem(b // 2, 2)
    y, z = d // 2, b // 4
    x = 2 * xh + xl
    sid = b - c + xl
    e = d - xl + c
    same = c == xl
    apart = jnp.logical_not(same)

    def home(state, slab):
        sp, ep = lax.rem(state, 2), lax.rem(slab, 2)
        return (state - sp + ep, slab - ep + sp)

    e_out = lax.rem(e + 2 * c - 1 + nd, nd)
    e_in = e + 1 - 2 * c

    def way(k, n):
        return min(k, n - k)

    around = [(kz, kx) for kz in range(nz) for kx in range(4) if kz or kx]
    around.sort(key=lambda k: -way(k[0], nz) - way(k[1], 4))
    column = [(ky, kc) for ky in range(ny) for kc in range(2) if ky or kc]
    column.sort(key=lambda k: -2 * way(k[0], ny) - k[1])

    def state_at(kz, kx):
        return lax.rem(z + kz, nz) * 4 + lax.rem(x + kx, 4)

    def slab_at(ky, kc):
        return lax.rem(y + ky, ny) * 2 + lax.rem(c + kc, 2)

    def await_all(buffer, semaphore):
        pltpu.make_async_copy(buffer, buffer, semaphore).wait()

    def chip(kz, kx):
        return home(state_at(kz, kx), e)

    barrier = pltpu.get_barrier_semaphore()

    @pl.when(apart)
    def _():
        pl.semaphore_signal(barrier, inc=1, device_id=(sid, e), device_id_type=MESH)

    beside_z = [chip(1, 0), chip(nz - 1, 0)]
    beside_x = [chip(0, 1), chip(0, 3)]
    beside_c = [home(sid, e_in)]
    for who in beside_x + beside_z + beside_c + [home(sid, e_out)]:
        pl.semaphore_signal(barrier, inc=1, device_id=who, device_id_type=MESH)
    greeted = jnp.where(same, 6, 7)

    rounds = [beside_z, beside_x, beside_x, beside_c]

    def tell(i):
        for who in rounds[i]:
            pl.semaphore_signal(told.at[i], inc=1, device_id=who, device_id_type=MESH)

    def hear(i):
        pl.semaphore_wait(told.at[i], len(rounds[i]))

    def part(j, side):
        if j < STRIPS:
            return pl.ds(edge * side, HALO), pl.ds(j * strip, strip)
        if j == STRIPS:
            return pl.ds(edge * (1 - side), HALO), pl.ds(0, gy)
        return pl.ds(HALO, planes - 2 * HALO), pl.ds((j - STRIPS - 1) * strip, strip)

    def part_v(j, side):
        if j == 0:
            return pl.ds(edge * side, HALO)
        return pl.ds(HALO * (1 - side), edge)

    def shifted(rows):
        return pl.ds(HALO + rows.start, rows.size)

    def local_x(j):
        at, rows = part(j, c)
        return pltpu.make_async_copy(x_in.at[0, at, rows], field[0].at[shifted(at), rows],
                                     r_x.at[j])

    def local_v(j):
        at = part_v(j, c)
        return pltpu.make_async_copy(v_in.at[at], pot.at[at], r_v.at[j])

    @pl.when(same)
    def _():
        for j in range(2 * STRIPS + 1):
            local_x(j).start()
        for j in range(2):
            local_v(j).start()

    pl.semaphore_wait(barrier, greeted)

    def swap(j):
        at, rows = part(j, xl)
        return pltpu.make_async_remote_copy(
            src_ref=x_in.at[0, at, rows], dst_ref=field[0].at[shifted(at), rows],
            send_sem=s_x.at[j], recv_sem=r_x.at[j], device_id=(sid, e), device_id_type=MESH)

    def give_v(j):
        at = part_v(j, c)
        return pltpu.make_async_remote_copy(
            src_ref=v_in.at[at], dst_ref=pot.at[at], send_sem=s_v.at[j], recv_sem=r_v.at[j],
            device_id=(b + 2 - 4 * xh, d + 1 - 2 * xl), device_id_type=MESH)

    @pl.when(apart)
    def _():
        for j in range(2 * STRIPS + 1):
            swap(j).start()

    @pl.when(same)
    def _():
        for j in range(2):
            give_v(j).start()

    tell(0)
    high, low = circulant(gz)
    wz[0:gz, 0:gz] = high
    wz[gz:, 0:gz] = high
    wz[0:gz, gz:] = low
    wz[gz:, gz:] = jnp.zeros_like(low)
    high, low = circulant(gy)
    wy[0:gy, 0:gy] = high
    wy[0:gy, gy:] = high
    wy[gy:, 0:gy] = low
    wy[gy:, gy:] = jnp.zeros_like(low)

    def send_outer(k, j):
        rows = pl.ds(j * strip, strip)
        return pltpu.make_async_remote_copy(
            src_ref=field[k].at[pl.ds(HALO + edge * c, HALO), rows],
            dst_ref=field[k].at[pl.ds((HALO + planes) * (1 - c), HALO), rows],
            send_sem=s_o.at[k, j], recv_sem=r_o.at[k, j],
            device_id=home(sid, e_out), device_id_type=MESH)

    def send_inner(k):
        return pltpu.make_async_remote_copy(
            src_ref=field[k].at[pl.ds(HALO + edge * (1 - c), HALO)],
            dst_ref=field[k].at[pl.ds((HALO + planes) * c, HALO)],
            send_sem=s_i.at[k], recv_sem=r_i.at[k],
            device_id=home(sid, e_in), device_id_type=MESH)

    def own(rank):
        return rank + c * (planes - 1 - 2 * rank)

    def turned(k, rank, n, terms):
        high, low = [], []
        for t in range(n):
            h, l = halves(field[k - 1][HALO + own(rank + t)])
            high.append(h)
            low.append(l)
        along_z = jnp.dot(
            jnp.concatenate([jnp.concatenate([h, l], 1) for h, l in zip(high, low)], 0),
            wz[...], preferred_element_type=F32)
        along_y = jnp.dot(
            wy[...], jnp.concatenate([jnp.concatenate(high, 1), jnp.concatenate(low, 1)], 0),
            preferred_element_type=F32)
        for t in range(n):
            terms[t] = (along_z[t * gy:(t + 1) * gy, 0:gz] + along_z[t * gy:(t + 1) * gy, gz:]
                        + along_y[0:gy, t * gz:(t + 1) * gz] + along_y[gy:, t * gz:(t + 1) * gz])

    def planes_of(k, rank, n, terms, top=0, bottom=None):
        scale, weight = plan[k - 1]
        shift = -(centre + 1.5 * COEFFS[0]) * scale
        factor = -0.5 * scale
        for r0 in range(top, gy if bottom is None else bottom, 16):
            rows = pl.ds(r0, min(16, strip))
            first = rank - HALO if rank else 0
            near = {j: field[k - 1][HALO + own(j), rows] for j in range(first, rank + n + HALO)}
            for t in range(n):
                here = rank + t
                value = (pot[own(here), rows] * scale + shift) * near[here]
                value = value + factor * terms[t, rows]
                for offset in range(1, HALO + 1):
                    side = near[here + offset]
                    if here - offset in near:
                        side = side + near[here - offset]
                    value = value + (factor * COEFFS[offset]) * side
                if k > 1:
                    value = value - weight * field[k - 2][HALO + own(here), rows]
                field[k][HALO + own(here), rows] = value

    def with_halo(k, j):
        factor = -0.5 * plan[k - 1][0]
        planes_of(k, 0, HALO, t_out, j * strip, (j + 1) * strip)
        send_outer(k - 1, j).wait_recv()
        for r0 in range(0, strip, 16):
            rows = pl.ds(j * strip + r0, min(16, strip))
            near = [field[k - 1][HALO + own(-offset), rows] for offset in range(1, HALO + 1)]
            for rank in range(HALO):
                at = HALO + own(rank)
                value = field[k][at, rows]
                for offset in range(rank + 1, HALO + 1):
                    value = value + (factor * COEFFS[offset]) * near[offset - rank - 1]
                field[k][at, rows] = value
        if k < STEPS:
            send_outer(k, j).start()

    body = planes - 2 * HALO
    t_mid, t_inner = t_in.at[pl.ds(0, body)], t_in.at[pl.ds(body, HALO)]

    def turn_outer(k):
        turned(k, 0, HALO, t_out)

    def turn_inner(k):
        turned(k, HALO, body, t_mid)
        turned(k, edge, HALO, t_inner)

    first, second, whole = pl.ds(0, half), pl.ds(half, half), pl.ds(0, gy)

    def dealt(rank):
        return lax.rem(rank, 4) * 4 + lax.rem(lax.rem(rank, 4) + rank // 4 + 2 * c, 4)

    my_rank = 4 * lax.rem(x - z + 8 - 2 * c, 4) + z
    my_plane = own(my_rank)

    def spread(rank, rows, j):
        to = dealt(rank)
        return pltpu.make_async_remote_copy(
            src_ref=field[STEPS].at[HALO + own(rank), rows], dst_ref=recv.at[sid, rows],
            send_sem=s_f.at[0], recv_sem=r_f.at[j],
            device_id=home(to, e), device_id_type=MESH)

    def spread_ranks(rank, n, rows, j, act):
        for k in range(n):
            at = rank + lax.rem(k + z + x, n)

            @pl.when(at != my_rank)
            def _():
                act(spread(at, rows, j))

    def start(copy):
        copy.start()

    for j in range(STRIPS):
        local_x(j).wait()
        send_outer(0, j).start()
    turn_outer(1)
    local_v(0).wait()
    local_x(STRIPS).wait()
    send_inner(0).start()
    turned(1, edge, HALO, t_inner)
    for j in range(STRIPS):
        local_x(STRIPS + 1 + j).wait()
        with_halo(1, j)
    hear(0)
    tell(1)
    local_v(1).wait()
    send_inner(0).wait_recv()
    planes_of(1, edge, HALO, t_inner)
    send_inner(1).start()
    turned(1, HALO, body, t_mid)
    planes_of(1, HALO, body, t_mid)
    turn_outer(2)

    for k in range(2, STEPS):
        last = k == STEPS - 1
        if k > 2:
            turn_outer(k)
        with_halo(k, 0)
        hear(k - 1)
        tell(k)
        if k == 2:
            turn_inner(k)
        planes_of(k, HALO, body, t_mid)
        if not last:
            with_halo(k, 1)
        send_inner(k - 1).wait_recv()
        planes_of(k, edge, HALO, t_inner)
        send_inner(k).start()
        if last:
            with_halo(k, 1)
            turn_inner(k + 1)
        for j in range(2, STRIPS - 1):
            with_halo(k, j)
        if not last:
            turn_inner(k + 1)
            with_halo(k, STRIPS - 1)

    hear(3)

    deep = HALO - EARLY
    send_inner(STEPS - 1).wait_recv()
    planes_of(STEPS, planes - EARLY, EARLY, t_inner.at[pl.ds(deep, EARLY)])
    spread_ranks(planes - EARLY, EARLY, whole, 0, start)
    with_halo(STEPS - 1, STRIPS - 1)
    planes_of(STEPS, HALO, body + deep, t_in.at[pl.ds(0, body + deep)])
    spread_ranks(HALO, body + deep, whole, 0, start)
    turn_outer(STEPS)
    for j in range(STRIPS // 2):
        with_halo(STEPS, j)
    spread_ranks(0, HALO, first, 0, start)
    for j in range(STRIPS // 2, STRIPS):
        with_halo(STEPS, j)
    spread_ranks(0, HALO, second, 1, start)
    recv[pl.ds(sid, 1)] = field[STEPS][pl.ds(HALO + my_plane, 1)]

    tall = nb * 8
    wide = half // 8 * gz
    late = my_rank < HALO

    def arrived(rows, j):
        await_all(recv.at[pl.ds(0, nb - 1), rows], r_f.at[j])

    def products(j):
        high, low = [], []
        for g in range(half // 8):
            h, l = halves(recv[:, j * half + 8 * g:j * half + 8 * g + 8, :].reshape(tall, gz))
            high.append(h)
            low.append(l)
        both = jnp.concatenate([jnp.concatenate(high, 1), jnp.concatenate(low, 1)], 0)
        split[:, j * wide:(j + 1) * wide] = both
        return lax.dot_general(both, both, (((1,), (1,)), ((), ())), preferred_element_type=F32)

    @pl.when(late)
    def _():
        arrived(first, 0)

    @pl.when(jnp.logical_not(late))
    def _():
        arrived(whole, 0)

    total = products(0)

    @pl.when(late)
    def _():
        arrived(second, 1)

    total = total + products(1)
    total = total[0:tall, 0:tall] + total[0:tall, tall:] + total[tall:, 0:tall] + total[tall:, tall:]
    at_row = lax.broadcasted_iota(jnp.int32, (tall, tall), 0)
    at_col = lax.broadcasted_iota(jnp.int32, (tall, tall), 1)
    match = lax.rem(at_row, 8) == lax.rem(at_col, 8)
    total = jnp.where(match, total, 0.0).reshape(nb, 8, tall).sum(axis=1)
    total = total + pltpu.roll(total, tall - 4, 1)
    lower = lax.rem(lax.broadcasted_iota(jnp.int32, (nb // 2, tall), 1), 8) < 4
    gb[pl.ds(e, 1)] = jnp.where(
        lower, total[0:nb // 2], pltpu.roll(total[nb // 2:], 4, 1))[None]

    def share_b(ky, kc):
        to = slab_at(ky, kc)
        return pltpu.make_async_remote_copy(
            src_ref=gb.at[e], dst_ref=gb.at[e], send_sem=s_b.at[0], recv_sem=r_b.at[0],
            device_id=home(sid, to), device_id_type=MESH)

    for ky, kc in column:
        share_b(ky, kc).start()
    await_all(gb.at[pl.ds(0, nd - 1)], r_b.at[0])
    ga[pl.ds(sid, 1)] = jnp.sum(gb[...], axis=0, keepdims=True)

    def share_a(kz, kx):
        to = state_at(kz, kx)
        return pltpu.make_async_remote_copy(
            src_ref=ga.at[sid], dst_ref=ga.at[sid], send_sem=s_a.at[0], recv_sem=r_a.at[0],
            device_id=home(to, e), device_id_type=MESH)

    for kz, kx in around:
        share_a(kz, kx).start()
    same_state = (at_row // 8 == at_col // 8).astype(F32)
    await_all(ga.at[pl.ds(0, nb - 1)], r_a.at[0])

    whole_sum = jnp.sum(ga[...], axis=0) / float(planes * nd * gy * gz)
    whole_sum = jnp.concatenate(
        [jnp.where(lower, whole_sum, 0.0), jnp.where(lower, 0.0, whole_sum)], 0)
    matrix = jnp.dot(whole_sum, same_state, precision=lax.Precision.HIGHEST,
                     preferred_element_type=F32)

    sub = lax.broadcasted_iota(jnp.int32, (nb, tall), 0)
    lane = lax.broadcasted_iota(jnp.int32, (nb, tall), 1)
    work = matrix
    inverse = (sub == lane // 8).astype(F32)
    for k in range(nb - 1):
        factor = work[:, 8 * k:8 * k + 1] / work[k:k + 1, 8 * k:8 * k + 1]
        factor = jnp.where(sub > k, factor, 0.0)
        work = work - factor * work[k:k + 1, :]
        inverse = inverse - factor * inverse[k:k + 1, :]
    diagonal = jnp.sum(jnp.where(lane == 8 * sub, work, 0.0), axis=1, keepdims=True)
    inverse = inverse / jnp.sqrt(diagonal)

    inverse = jnp.broadcast_to(inverse[:, None, :], (nb, 8, tall)).reshape(tall, tall)
    high, low = halves(jnp.where(match, inverse, 0.0))
    left = jnp.concatenate([jnp.concatenate([high, high], 1),
                            jnp.concatenate([low, jnp.zeros_like(low)], 1)], 0)

    back = [(kz, h, t) for kz in range(nz) for h in range(2) for t in range(2)]
    back.sort(key=lambda k: (-way(k[0], nz) - k[1], -k[2]))

    piece = gy // PIECES
    span = piece // 8 * gz

    def give_back(kz, h, t, j):
        state = lax.rem(z + kz, nz) * 4 + lax.rem(xh + h, 2) * 2 + lax.rem(c + t, 2)
        rows = pl.ds(j * piece, piece)
        return pltpu.make_async_remote_copy(
            src_ref=ortho.at[state, rows], dst_ref=out.at[0, my_plane, rows],
            send_sem=s_r.at[0], recv_sem=r_r.at[0], device_id=(state, e),
            device_id_type=MESH)

    def own_back(j):
        rows = pl.ds(j * piece, piece)
        return pltpu.make_async_copy(
            ortho.at[b, rows], out.at[0, my_plane, rows], r_r.at[0])

    for j in range(PIECES):
        value = jnp.dot(left, split[:, j * span:(j + 1) * span], preferred_element_type=F32)
        for g in range(piece // 8):
            at = slice(g * gz, (g + 1) * gz)
            ortho[:, j * piece + 8 * g:j * piece + 8 * g + 8, :] = (
                value[0:tall, at] + value[tall:, at]).reshape(nb, 8, gz)
        for item in back[:-1]:
            give_back(*item, j).start()

        @pl.when(same)
        def _():
            own_back(j).start()

        @pl.when(apart)
        def _():
            give_back(*back[-1], j).start()

    pick_row = lax.broadcasted_iota(jnp.int32, (tall, nb), 0)
    pick_col = lax.broadcasted_iota(jnp.int32, (tall, nb), 1)
    corr[...] = jnp.dot(matrix, (pick_row == 8 * pick_col).astype(F32),
                        precision=lax.Precision.HIGHEST, preferred_element_type=F32)

    @pl.when(apart)
    def _():
        for j in range(2 * STRIPS + 1):
            swap(j).wait_send()

    @pl.when(same)
    def _():
        for j in range(2):
            give_v(j).wait_send()

    for k in range(STEPS):
        for j in range(STRIPS):
            send_outer(k, j).wait_send()
        send_inner(k).wait_send()
    await_all(recv.at[pl.ds(0, nb - 1)], s_f.at[0])
    await_all(gb.at[pl.ds(0, nd - 1)], s_b.at[0])
    await_all(ga.at[pl.ds(0, nb - 1)], s_a.at[0])
    await_all(ortho.at[pl.ds(0, nb - 1)], s_r.at[0])

    @pl.when(apart)
    def _():
        await_all(ortho.at[0], s_r.at[0])

    await_all(out.at[0], r_r.at[0])


def shards(orbitals, potential):
    nb, nd = lax.axis_size("band"), lax.axis_size("dom")
    planes, gy, gz = potential.shape
    tall = nb * 8
    dma = pltpu.SemaphoreType.DMA
    any_space = pl.BlockSpec(memory_space=pl.ANY)
    hbm = pl.BlockSpec(memory_space=pltpu.HBM)
    return pl.pallas_call(
        lambda *refs: kernel(nb, nd, *refs),
        out_shape=(jax.ShapeDtypeStruct(orbitals.shape, F32),
                   jax.ShapeDtypeStruct((nb, nb), F32)),
        in_specs=[hbm, hbm],
        out_specs=(any_space, pl.BlockSpec(memory_space=pltpu.VMEM)),
        scratch_shapes=[
            *[pltpu.VMEM((planes + 2 * HALO, gy, gz), F32) for _ in range(STEPS + 1)],
            pltpu.VMEM((planes, gy, gz), F32),
            pltpu.VMEM((2 * gz, 2 * gz), BF16),
            pltpu.VMEM((2 * gy, 2 * gy), BF16),
            pltpu.VMEM((HALO, gy, gz), F32),
            pltpu.VMEM((planes - HALO, gy, gz), F32),
            pltpu.VMEM((nb, gy, gz), F32),
            pltpu.VMEM((2 * tall, gy // 8 * gz), BF16),
            pltpu.VMEM((nb, gy, gz), F32),
            pltpu.VMEM((nb, nb // 2, tall), F32),
            pltpu.VMEM((nd, nb // 2, tall), F32),
            dma((2 * STRIPS + 1,)), dma((2 * STRIPS + 1,)),
            dma((2,)), dma((2,)),
            dma((STEPS, STRIPS)), dma((STEPS, STRIPS)),
            dma((STEPS,)), dma((STEPS,)),
            dma((1,)), dma((2,)),
            dma((1,)), dma((1,)),
            dma((1,)), dma((1,)),
            dma((1,)), dma((1,)),
            pltpu.SemaphoreType.REGULAR((4,)),
        ],
        compiler_params=pltpu.CompilerParams(
            collective_id=0, has_side_effects=True, vmem_limit_bytes=52 * 1024 * 1024),
        cost_estimate=pl.CostEstimate(flops=2 * 10**9, bytes_accessed=4 * 10**6,
                                      transcendentals=0),
    )(orbitals, potential)


def solution(mesh):
    placed = (P("band", "dom", None, None), P("dom", None, None))
    return jax.shard_map(
        shards,
        mesh=mesh,
        in_specs=placed,
        out_specs=(P("band", "dom", None, None), P()),
        check_vma=False,
    )
```

```python
import jax
import jax.numpy as jnp
from jax import lax
from jax.experimental import pallas as pl
from jax.experimental.pallas import tpu as pltpu
from jax.sharding import PartitionSpec as P

STEPS = 4
COEFFS = (
    -5369.0 / 1800.0,
    12.0 / 7.0,
    -15.0 / 56.0,
    10.0 / 189.0,
    -1.0 / 112.0,
    2.0 / 1925.0,
    -1.0 / 16632.0,
)
LOWER_EDGE = -3.5
CUT_EDGE = 0.5
UPPER_EDGE = 11.0
HALO = 6
STRIPS = 4
EARLY = 4
PIECES = 2
MESH = pl.DeviceIdType.MESH
F32 = jnp.float32
BF16 = jnp.bfloat16


def recurrence(count):
    half_width = (UPPER_EDGE - CUT_EDGE) / 2.0
    centre = (UPPER_EDGE + CUT_EDGE) / 2.0
    sigma_now = half_width / (LOWER_EDGE - centre)
    gamma_value = 2.0 / sigma_now
    plan = [(sigma_now / half_width, 0.0)]
    for number in range(count - 1):
        sigma_next = 1.0 / (gamma_value - sigma_now)
        plan.append((2.0 * sigma_next / half_width, sigma_now * sigma_next))
        sigma_now = sigma_next
    return (centre, plan)


def halves(value):
    high = value.astype(BF16)
    return high, (value - high.astype(F32)).astype(BF16)


def circulant(size):
    row = lax.broadcasted_iota(jnp.int32, (size, size), 0)
    col = lax.broadcasted_iota(jnp.int32, (size, size), 1)
    gap = jnp.abs(row - col)
    gap = jnp.minimum(gap, size - gap)
    value = jnp.zeros((size, size), F32)
    for offset in range(1, HALO + 1):
        value = jnp.where(gap == offset, COEFFS[offset], value)
    return halves(value)


def kernel(nb, nd, x_in, v_in, out, corr, field0, field1, field2, field3, field4, pot, wz, wy, t_out, t_in, recv, split, ortho,
           ga, gb, s_x, r_x, s_v, r_v, s_o, r_o, s_i, r_i, s_f, r_f, s_a, r_a, s_b, r_b,
           s_r, r_r, told):
    field = (field0, field1, field2, field3, field4)
    planes, gy, gz = v_in.shape
    edge = planes - HALO
    nz, ny = nb // 4, nd // 2
    strip = gy // STRIPS
    half = gy // 2
    centre, plan = recurrence(STEPS)
    b, d = lax.axis_index("band"), lax.axis_index("dom")
    c, xl = lax.rem(b, 2), lax.rem(d, 2)
    xh = lax.rem(b // 2, 2)
    y, z = d // 2, b // 4
    x = 2 * xh + xl
    sid = b - c + xl
    e = d - xl + c
    same = c == xl
    apart = jnp.logical_not(same)

    def home(state, slab):
        sp, ep = lax.rem(state, 2), lax.rem(slab, 2)
        return (state - sp + ep, slab - ep + sp)

    e_out = lax.rem(e + 2 * c - 1 + nd, nd)
    e_in = e + 1 - 2 * c

    def way(k, n):
        return min(k, n - k)

    around = [(kz, kx) for kz in range(nz) for kx in range(4) if kz or kx]
    around.sort(key=lambda k: -way(k[0], nz) - way(k[1], 4))
    column = [(ky, kc) for ky in range(ny) for kc in range(2) if ky or kc]
    column.sort(key=lambda k: -2 * way(k[0], ny) - k[1])

    def state_at(kz, kx):
        return lax.rem(z + kz, nz) * 4 + lax.rem(x + kx, 4)

    def slab_at(ky, kc):
        return lax.rem(y + ky, ny) * 2 + lax.rem(c + kc, 2)

    def await_all(buffer, semaphore):
        pltpu.make_async_copy(buffer, buffer, semaphore).wait()

    def chip(kz, kx):
        return home(state_at(kz, kx), e)

    barrier = pltpu.get_barrier_semaphore()

    @pl.when(apart)
    def _():
        pl.semaphore_signal(barrier, inc=1, device_id=(sid, e), device_id_type=MESH)

    beside_z = [chip(1, 0), chip(nz - 1, 0)]
    beside_x = [chip(0, 1), chip(0, 3)]
    beside_c = [home(sid, e_in)]
    for who in beside_x + beside_z + beside_c + [home(sid, e_out)]:
        pl.semaphore_signal(barrier, inc=1, device_id=who, device_id_type=MESH)
    greeted = jnp.where(same, 6, 7)

    rounds = [beside_z, beside_x, beside_x, beside_c]

    def tell(i):
        for who in rounds[i]:
            pl.semaphore_signal(told.at[i], inc=1, device_id=who, device_id_type=MESH)

    def hear(i):
        pl.semaphore_wait(told.at[i], len(rounds[i]))

    def part(j, side):
        if j < STRIPS:
            return pl.ds(edge * side, HALO), pl.ds(j * strip, strip)
        if j == STRIPS:
            return pl.ds(edge * (1 - side), HALO), pl.ds(0, gy)
        return pl.ds(HALO, planes - 2 * HALO), pl.ds((j - STRIPS - 1) * strip, strip)

    def part_v(j, side):
        if j == 0:
            return pl.ds(edge * side, HALO)
        return pl.ds(HALO * (1 - side), edge)

    def shifted(rows):
        return pl.ds(HALO + rows.start, rows.size)

    def local_x(j):
        at, rows = part(j, c)
        return pltpu.make_async_copy(x_in.at[0, at, rows], field[0].at[shifted(at), rows],
                                     r_x.at[j])

    def local_v(j):
        at = part_v(j, c)
        return pltpu.make_async_copy(v_in.at[at], pot.at[at], r_v.at[j])

    @pl.when(same)
    def _():
        for j in range(2 * STRIPS + 1):
            local_x(j).start()
        for j in range(2):
            local_v(j).start()

    pl.semaphore_wait(barrier, greeted)

    def swap(j):
        at, rows = part(j, xl)
        return pltpu.make_async_remote_copy(
            src_ref=x_in.at[0, at, rows], dst_ref=field[0].at[shifted(at), rows],
            send_sem=s_x.at[j], recv_sem=r_x.at[j], device_id=(sid, e), device_id_type=MESH)

    def give_v(j):
        at = part_v(j, c)
        return pltpu.make_async_remote_copy(
            src_ref=v_in.at[at], dst_ref=pot.at[at], send_sem=s_v.at[j], recv_sem=r_v.at[j],
            device_id=(b + 2 - 4 * xh, d + 1 - 2 * xl), device_id_type=MESH)

    @pl.when(apart)
    def _():
        for j in range(2 * STRIPS + 1):
            swap(j).start()

    @pl.when(same)
    def _():
        for j in range(2):
            give_v(j).start()

    tell(0)
    high, low = circulant(gz)
    wz[0:gz, 0:gz] = high
    wz[gz:, 0:gz] = high
    wz[0:gz, gz:] = low
    wz[gz:, gz:] = jnp.zeros_like(low)
    high, low = circulant(gy)
    wy[0:gy, 0:gy] = high
    wy[0:gy, gy:] = high
    wy[gy:, 0:gy] = low
    wy[gy:, gy:] = jnp.zeros_like(low)

    def send_outer(k, j):
        rows = pl.ds(j * strip, strip)
        return pltpu.make_async_remote_copy(
            src_ref=field[k].at[pl.ds(HALO + edge * c, HALO), rows],
            dst_ref=field[k].at[pl.ds((HALO + planes) * (1 - c), HALO), rows],
            send_sem=s_o.at[k], recv_sem=r_o.at[k, j],
            device_id=home(sid, e_out), device_id_type=MESH)

    def send_inner(k):
        return pltpu.make_async_remote_copy(
            src_ref=field[k].at[pl.ds(HALO + edge * (1 - c), HALO)],
            dst_ref=field[k].at[pl.ds((HALO + planes) * c, HALO)],
            send_sem=s_i.at[0], recv_sem=r_i.at[k],
            device_id=home(sid, e_in), device_id_type=MESH)

    def own(rank):
        return rank + c * (planes - 1 - 2 * rank)

    def turned(k, rank, n, terms):
        high, low = [], []
        for t in range(n):
            h, l = halves(field[k - 1][HALO + own(rank + t)])
            high.append(h)
            low.append(l)
        along_z = jnp.dot(
            jnp.concatenate([jnp.concatenate([h, l], 1) for h, l in zip(high, low)], 0),
            wz[...], preferred_element_type=F32)
        along_y = jnp.dot(
            wy[...], jnp.concatenate([jnp.concatenate(high, 1), jnp.concatenate(low, 1)], 0),
            preferred_element_type=F32)
        for t in range(n):
            terms[t] = (along_z[t * gy:(t + 1) * gy, 0:gz] + along_z[t * gy:(t + 1) * gy, gz:]
                        + along_y[0:gy, t * gz:(t + 1) * gz] + along_y[gy:, t * gz:(t + 1) * gz])

    def planes_of(k, rank, n, terms, top=0, bottom=None):
        scale, weight = plan[k - 1]
        shift = -(centre + 1.5 * COEFFS[0]) * scale
        factor = -0.5 * scale
        for r0 in range(top, gy if bottom is None else bottom, 32):
            rows = pl.ds(r0, 32)
            first = rank - HALO if rank else 0
            near = {j: field[k - 1][HALO + own(j), rows] for j in range(first, rank + n + HALO)}
            for t in range(n):
                here = rank + t
                value = (pot[own(here), rows] * scale + shift) * near[here]
                value = value + factor * terms[t, rows]
                for offset in range(1, HALO + 1):
                    side = near[here + offset]
                    if here - offset in near:
                        side = side + near[here - offset]
                    value = value + (factor * COEFFS[offset]) * side
                if k > 1:
                    value = value - weight * field[k - 2][HALO + own(here), rows]
                field[k][HALO + own(here), rows] = value

    def with_halo(k, j):
        factor = -0.5 * plan[k - 1][0]
        planes_of(k, 0, HALO, t_out, j * strip, (j + 1) * strip)
        send_outer(k - 1, j).wait_recv()
        for r0 in range(0, strip, 16):
            rows = pl.ds(j * strip + r0, min(16, strip))
            near = [field[k - 1][HALO + own(-offset), rows] for offset in range(1, HALO + 1)]
            for rank in range(HALO):
                at = HALO + own(rank)
                value = field[k][at, rows]
                for offset in range(rank + 1, HALO + 1):
                    value = value + (factor * COEFFS[offset]) * near[offset - rank - 1]
                field[k][at, rows] = value
        if k < STEPS:
            send_outer(k, j).start()

    body = planes - 2 * HALO
    t_mid, t_inner = t_in.at[pl.ds(0, body)], t_in.at[pl.ds(body, HALO)]

    def turn_outer(k):
        turned(k, 0, HALO, t_out)

    def turn_inner(k):
        turned(k, HALO, body, t_mid)
        turned(k, edge, HALO, t_inner)

    first, second, whole = pl.ds(0, half), pl.ds(half, half), pl.ds(0, gy)

    def dealt(rank):
        return lax.rem(rank, 4) * 4 + lax.rem(lax.rem(rank, 4) + rank // 4 + 2 * c, 4)

    my_rank = 4 * lax.rem(x - z + 8 - 2 * c, 4) + z
    my_plane = own(my_rank)

    def spread(rank, rows, j):
        to = dealt(rank)
        return pltpu.make_async_remote_copy(
            src_ref=field[STEPS].at[HALO + own(rank), rows], dst_ref=recv.at[sid, rows],
            send_sem=s_f.at[0], recv_sem=r_f.at[j],
            device_id=home(to, e), device_id_type=MESH)

    def spread_ranks(rank, n, rows, j, act):
        for k in range(n):
            at = rank + lax.rem(k + z + x, n)

            @pl.when(at != my_rank)
            def _():
                act(spread(at, rows, j))

    def start(copy):
        copy.start()

    for j in range(STRIPS):
        local_x(j).wait()
        send_outer(0, j).start()
    turn_outer(1)
    local_v(0).wait()
    local_x(STRIPS).wait()
    send_inner(0).start()
    turned(1, edge, HALO, t_inner)
    for j in range(STRIPS):
        local_x(STRIPS + 1 + j).wait()
        with_halo(1, j)
    hear(0)
    tell(1)
    local_v(1).wait()
    send_inner(0).wait_recv()
    planes_of(1, edge, HALO, t_inner)
    send_inner(1).start()
    turned(1, HALO, body, t_mid)
    planes_of(1, HALO, body, t_mid)
    turn_outer(2)

    for k in range(2, STEPS):
        last = k == STEPS - 1
        if k > 2:
            turn_outer(k)
        with_halo(k, 0)
        hear(k - 1)
        tell(k)
        if k == 2:
            turn_inner(k)
        planes_of(k, HALO, body, t_mid)
        if not last:
            with_halo(k, 1)
        send_inner(k - 1).wait_recv()
        planes_of(k, edge, HALO, t_inner)
        send_inner(k).start()
        if last:
            with_halo(k, 1)
            turn_inner(k + 1)
        for j in range(2, STRIPS - 1):
            with_halo(k, j)
        if not last:
            turn_inner(k + 1)
            with_halo(k, STRIPS - 1)

    hear(3)

    deep = HALO - EARLY
    send_inner(STEPS - 1).wait_recv()
    planes_of(STEPS, planes - EARLY, EARLY, t_inner.at[pl.ds(deep, EARLY)])
    spread_ranks(planes - EARLY, EARLY, whole, 0, start)
    with_halo(STEPS - 1, STRIPS - 1)
    planes_of(STEPS, HALO, body + deep, t_in.at[pl.ds(0, body + deep)])
    spread_ranks(HALO, body + deep, whole, 0, start)
    turn_outer(STEPS)
    for j in range(STRIPS // 2):
        with_halo(STEPS, j)
    spread_ranks(0, HALO, first, 0, start)
    for j in range(STRIPS // 2, STRIPS):
        with_halo(STEPS, j)
    spread_ranks(0, HALO, second, 1, start)
    recv[pl.ds(sid, 1)] = field[STEPS][pl.ds(HALO + my_plane, 1)]

    tall = nb * 8
    wide = half // 8 * gz
    late = my_rank < HALO

    def arrived(rows, j):
        await_all(recv.at[pl.ds(0, nb - 1), rows], r_f.at[j])

    def products(j):
        high, low = [], []
        for g in range(half // 8):
            h, l = halves(recv[:, j * half + 8 * g:j * half + 8 * g + 8, :].reshape(tall, gz))
            high.append(h)
            low.append(l)
        both = jnp.concatenate([jnp.concatenate(high, 1), jnp.concatenate(low, 1)], 0)
        split[:, j * wide:(j + 1) * wide] = both
        return lax.dot_general(both, both, (((1,), (1,)), ((), ())), preferred_element_type=F32)

    @pl.when(late)
    def _():
        arrived(first, 0)

    @pl.when(jnp.logical_not(late))
    def _():
        arrived(whole, 0)

    total = products(0)

    @pl.when(late)
    def _():
        arrived(second, 1)

    total = total + products(1)
    total = total[0:tall, 0:tall] + total[0:tall, tall:] + total[tall:, 0:tall] + total[tall:, tall:]
    at_row = lax.broadcasted_iota(jnp.int32, (tall, tall), 0)
    at_col = lax.broadcasted_iota(jnp.int32, (tall, tall), 1)
    match = lax.rem(at_row, 8) == lax.rem(at_col, 8)
    total = jnp.where(match, total, 0.0).reshape(nb, 8, tall).sum(axis=1)
    total = total + pltpu.roll(total, tall - 4, 1)
    lower = lax.rem(lax.broadcasted_iota(jnp.int32, (nb // 2, tall), 1), 8) < 4
    gb[pl.ds(e, 1)] = jnp.where(
        lower, total[0:nb // 2], pltpu.roll(total[nb // 2:], 4, 1))[None]

    def share_b(ky, kc):
        to = slab_at(ky, kc)
        return pltpu.make_async_remote_copy(
            src_ref=gb.at[e], dst_ref=gb.at[e], send_sem=s_b.at[0], recv_sem=r_b.at[0],
            device_id=home(sid, to), device_id_type=MESH)

    for ky, kc in column:
        share_b(ky, kc).start()
    await_all(gb.at[pl.ds(0, nd - 1)], r_b.at[0])
    ga[pl.ds(sid, 1)] = jnp.sum(gb[...], axis=0, keepdims=True)

    def share_a(kz, kx):
        to = state_at(kz, kx)
        return pltpu.make_async_remote_copy(
            src_ref=ga.at[sid], dst_ref=ga.at[sid], send_sem=s_a.at[0], recv_sem=r_a.at[0],
            device_id=home(to, e), device_id_type=MESH)

    for kz, kx in around:
        share_a(kz, kx).start()
    same_state = (at_row // 8 == at_col // 8).astype(F32)
    await_all(ga.at[pl.ds(0, nb - 1)], r_a.at[0])

    whole_sum = jnp.sum(ga[...], axis=0) / float(planes * nd * gy * gz)
    whole_sum = jnp.concatenate(
        [jnp.where(lower, whole_sum, 0.0), jnp.where(lower, 0.0, whole_sum)], 0)
    matrix = jnp.dot(whole_sum, same_state, precision=lax.Precision.HIGHEST,
                     preferred_element_type=F32)

    sub = lax.broadcasted_iota(jnp.int32, (nb, tall), 0)
    lane = lax.broadcasted_iota(jnp.int32, (nb, tall), 1)
    work = matrix
    inverse = (sub == lane // 8).astype(F32)
    for k in range(nb - 1):
        factor = work[:, 8 * k:8 * k + 1] / work[k:k + 1, 8 * k:8 * k + 1]
        factor = jnp.where(sub > k, factor, 0.0)
        work = work - factor * work[k:k + 1, :]
        inverse = inverse - factor * inverse[k:k + 1, :]
    diagonal = jnp.sum(jnp.where(lane == 8 * sub, work, 0.0), axis=1, keepdims=True)
    inverse = inverse / jnp.sqrt(diagonal)

    inverse = jnp.broadcast_to(inverse[:, None, :], (nb, 8, tall)).reshape(tall, tall)
    high, low = halves(jnp.where(match, inverse, 0.0))
    left = jnp.concatenate([jnp.concatenate([high, high], 1),
                            jnp.concatenate([low, jnp.zeros_like(low)], 1)], 0)

    back = [(kz, h, t) for kz in range(nz) for h in range(2) for t in range(2)]
    back.sort(key=lambda k: (-way(k[0], nz) - k[1], -k[2]))

    piece = gy // PIECES
    span = piece // 8 * gz

    def give_back(kz, h, t, j):
        state = lax.rem(z + kz, nz) * 4 + lax.rem(xh + h, 2) * 2 + lax.rem(c + t, 2)
        rows = pl.ds(j * piece, piece)
        return pltpu.make_async_remote_copy(
            src_ref=ortho.at[state, rows], dst_ref=out.at[0, my_plane, rows],
            send_sem=s_r.at[0], recv_sem=r_r.at[0], device_id=(state, e),
            device_id_type=MESH)

    def own_back(j):
        rows = pl.ds(j * piece, piece)
        return pltpu.make_async_copy(
            ortho.at[b, rows], out.at[0, my_plane, rows], r_r.at[0])

    for j in range(PIECES):
        value = jnp.dot(left, split[:, j * span:(j + 1) * span], preferred_element_type=F32)
        for g in range(piece // 8):
            at = slice(g * gz, (g + 1) * gz)
            ortho[:, j * piece + 8 * g:j * piece + 8 * g + 8, :] = (
                value[0:tall, at] + value[tall:, at]).reshape(nb, 8, gz)
        for item in back[:-1]:
            give_back(*item, j).start()

        @pl.when(same)
        def _():
            own_back(j).start()

        @pl.when(apart)
        def _():
            give_back(*back[-1], j).start()

    pick_row = lax.broadcasted_iota(jnp.int32, (tall, nb), 0)
    pick_col = lax.broadcasted_iota(jnp.int32, (tall, nb), 1)
    corr[...] = jnp.dot(matrix, (pick_row == 8 * pick_col).astype(F32),
                        precision=lax.Precision.HIGHEST, preferred_element_type=F32)

    @pl.when(apart)
    def _():
        for j in range(2 * STRIPS + 1):
            swap(j).wait_send()

    @pl.when(same)
    def _():
        for j in range(2):
            give_v(j).wait_send()

    for k in range(STEPS):
        await_all(field[k].at[pl.ds(0, HALO)], s_o.at[k])
    await_all(field[0].at[pl.ds(0, STEPS * HALO)], s_i.at[0])
    await_all(recv.at[pl.ds(0, nb - 1)], s_f.at[0])
    await_all(gb.at[pl.ds(0, nd - 1)], s_b.at[0])
    await_all(ga.at[pl.ds(0, nb - 1)], s_a.at[0])
    await_all(ortho.at[pl.ds(0, nb - 1)], s_r.at[0])

    @pl.when(apart)
    def _():
        await_all(ortho.at[0], s_r.at[0])

    await_all(out.at[0], r_r.at[0])


def shards(orbitals, potential):
    nb, nd = lax.axis_size("band"), lax.axis_size("dom")
    planes, gy, gz = potential.shape
    tall = nb * 8
    dma = pltpu.SemaphoreType.DMA
    any_space = pl.BlockSpec(memory_space=pl.ANY)
    hbm = pl.BlockSpec(memory_space=pltpu.HBM)
    return pl.pallas_call(
        lambda *refs: kernel(nb, nd, *refs),
        out_shape=(jax.ShapeDtypeStruct(orbitals.shape, F32),
                   jax.ShapeDtypeStruct((nb, nb), F32)),
        in_specs=[hbm, hbm],
        out_specs=(any_space, pl.BlockSpec(memory_space=pltpu.VMEM)),
        scratch_shapes=[
            *[pltpu.VMEM((planes + 2 * HALO, gy, gz), F32) for _ in range(STEPS + 1)],
            pltpu.VMEM((planes, gy, gz), F32),
            pltpu.VMEM((2 * gz, 2 * gz), BF16),
            pltpu.VMEM((2 * gy, 2 * gy), BF16),
            pltpu.VMEM((HALO, gy, gz), F32),
            pltpu.VMEM((planes - HALO, gy, gz), F32),
            pltpu.VMEM((nb, gy, gz), F32),
            pltpu.VMEM((2 * tall, gy // 8 * gz), BF16),
            pltpu.VMEM((nb, gy, gz), F32),
            pltpu.VMEM((nb, nb // 2, tall), F32),
            pltpu.VMEM((nd, nb // 2, tall), F32),
            dma((2 * STRIPS + 1,)), dma((2 * STRIPS + 1,)),
            dma((2,)), dma((2,)),
            dma((STEPS,)), dma((STEPS, STRIPS)),
            dma((1,)), dma((STEPS,)),
            dma((1,)), dma((2,)),
            dma((1,)), dma((1,)),
            dma((1,)), dma((1,)),
            dma((1,)), dma((1,)),
            pltpu.SemaphoreType.REGULAR((4,)),
        ],
        compiler_params=pltpu.CompilerParams(
            collective_id=0, has_side_effects=True, vmem_limit_bytes=52 * 1024 * 1024),
        cost_estimate=pl.CostEstimate(flops=2 * 10**9, bytes_accessed=4 * 10**6,
                                      transcendentals=0),
    )(orbitals, potential)


def solution(mesh):
    placed = (P("band", "dom", None, None), P("dom", None, None))
    return jax.shard_map(
        shards,
        mesh=mesh,
        in_specs=placed,
        out_specs=(P("band", "dom", None, None), P()),
        check_vma=False,
    )
```
